1024 devices in a mesh: expert: 64 (over z, core), tensor: 16 (over x, y).
Axes of the slice: x: 4, y: 4, z: 32, core: 2. Of those that a mesh axis runs over, the one named last changes fastest.
Arguments:
- grads: bfloat16 [16384, 7168], P('expert', 'tensor'), may hold values from -6 to 6
- routes: int32 [16384, 2], P('expert'), may hold values from 0 to 127, all different within a row; in each aligned block of 256 rows (0 to 255, 256 to 511, ...) at most 6 rows name the same one
- gates: float32 [16384, 2], P('expert'), may hold values from 0.2 to 1
- dense_down: bfloat16 [2432, 7168], P(None, 'tensor'), may hold values from -0.15625 to 0.15625
- dense_up: bfloat16 [7168, 2432], P('tensor'), may hold values from -0.0625 to 0.0625
- dense_act: bfloat16 [16384, 2432], P('expert', 'tensor'), may hold values from -6 to 6
- expert_down: bfloat16 [64, 1216, 7168], P('expert', None, 'tensor'), may hold values from -0.15625 to 0.15625
- expert_up: bfloat16 [64, 7168, 1216], P('expert', 'tensor'), may hold values from -0.0625 to 0.0625
- expert_act: bfloat16 [64, 384, 1216], P('expert', None, 'tensor'), may hold values from -6 to 6
Outputs:
- input_grad: bfloat16 [16384, 7168], P('expert', 'tensor')
The draws below stay inside these ranges and needn't reach their ends.
Inputs may be any that keep to these rules, and one draw needn't show every extreme that they name: `routes`: each row names two different experts; ids below 32 are held here. Within the 256 tokens of one index of expert no id is named more than 6 times, a bound that some block reaches.
All inputs are finite; a program needn't handle non-finite values.
Results may differ from the reference program's by a relative error of at most 0.02.
Values may be sent and summed in bfloat16 or wider, within the bound.
No kernel may reach another device: no remote copies, remote signals or barrier semaphores. Data moves between devices by JAX's collectives and lax.ppermute only.
A program may use at most 32 MiB of HBM per device.

```python
import math
import jax
import jax.numpy as jnp
import numpy as np
from jax import lax

D = 7168
HID = 2432
ALL_EXPERTS = 128
TOK_DEV = 256
CAP = 6
EXPERTS = 32
SLOTS = 384
TOKENS = 16384
N_TENSOR = 16


def raised(drawn, rng, source, target, blocks, factor):
    def block_of(position):
        return (jnp.arange(drawn.shape[position]) // (drawn.shape[position] // blocks)).reshape((-1,) + (1,) * (drawn.ndim - 1 - position))

    near = jax.random.permutation(rng, blocks)[block_of(target)]
    second = (block_of(target) + blocks // 2) % blocks
    return jnp.where((block_of(source) == near) | (block_of(source) == second), factor * drawn, drawn)


def levels(key, shape, split, smallest, largest):
    def one(dim, parts):
        steps = jax.random.uniform(jax.random.fold_in(jax.random.fold_in(key, 6), dim), (parts,), jnp.float32, smallest / len(split), largest / len(split))
        return jnp.repeat(jnp.exp(steps), shape[dim] // parts).reshape((-1,) + (1,) * (len(shape) - dim - 1))

    level = one(*split[0])
    for cut in split[1:]:
        level = level * one(*cut)
    return level


def shared_out(rng, own, number, rows, count, top, most, lean):
    ranking = jax.random.permutation(rng, count)
    packed, usual = portions_of(count, rows * top, most, lean, True), portions_of(count, rows * top, most, lean, False)
    places = jnp.arange(count)

    def named(lengths, turn):
        used = int((lengths > 0).sum())
        fixed = max(1, used // 4)
        moved = fixed + (places - fixed + turn * (used - fixed)) % max(1, count - fixed)
        return jnp.zeros((count,), jnp.int32).at[ranking[jnp.where(places < fixed, places, moved)]].set(jnp.asarray(lengths, jnp.int32))

    lengths = jnp.where(number % 4 == 0, named(packed, number // 4), named(usual, number - number // 4 - 1))
    mixed = jax.random.permutation(jax.random.fold_in(own, 3), count)
    donor, sink = mixed[0:count // 2 * 2:2], mixed[1:count // 2 * 2:2]
    slack = jnp.minimum(lengths[donor] - 1, most - lengths[sink]) // 2
    slack = jnp.where((donor == ranking[0]) | (sink == ranking[0]) | (lengths[sink] == 0), 0, jnp.maximum(slack, 0))
    moved = jax.random.randint(jax.random.fold_in(own, 4), (count // 2,), 0, 1 << 20) % (slack + 1)
    lengths = lengths.at[donor].add(-moved).at[sink].add(moved)
    items = jnp.searchsorted(jnp.cumsum(lengths), jnp.arange(rows * top), side="right").astype(jnp.int32)
    grid = items.reshape(top, rows).T
    grid = grid[jax.random.permutation(jax.random.fold_in(own, 1), rows)]
    turn = jax.random.randint(jax.random.fold_in(own, 2), (rows, 1), 0, top)
    return jnp.take_along_axis(grid, (jnp.arange(top)[None, :] + turn) % top, axis=1)


def portions_of(amount, total, bound, skew, full):
    loads = [(1 << 20) // math.isqrt(rank ** skew) + 1 for rank in range(1, amount + 1)]
    largest = bound if full else min(bound, max(-(-total // amount), total * loads[0] // sum(loads)))
    least = 1 if total - largest >= amount - 1 else 0
    counts, spare = [largest] + [least] * (amount - 1), total - largest - least * (amount - 1)
    while spare > 0:
        free = [i for i in range(1, amount) if counts[i] < largest] or [i for i in range(1, amount) if counts[i] < bound]
        mass, budget = sum([loads[i] for i in free]), spare
        for i in free:
            extra = min(bound - counts[i], max(1, budget * loads[i] // mass), spare)
            counts[i] = counts[i] + extra
            spare = spare - extra
    return np.array(counts)


def bell_draw(stream_key, extent, scale, reach, shards=(), held_as=jnp.bfloat16):
    drawn = scale * jax.random.normal(stream_key, extent, jnp.float32)
    if shards:
        drawn = drawn * levels(stream_key, extent, shards, -0.22, 0.18)
    return jnp.clip(drawn, -reach, reach).astype(held_as)


def gaussian_with(own_key, shape, deviation, most, pieces, heavy, held_as=jnp.bfloat16):
    entries = deviation * jax.random.normal(own_key, shape, jnp.float32)
    if pieces:
        entries = entries * levels(own_key, shape, pieces, -0.22, 0.18)
    return jnp.clip(raised(entries, jax.random.fold_in(own_key, 3), *heavy), -most, most).astype(held_as)


def setup_inputs(seed: int = 0) -> dict:
    seeds = jax.random.split(jax.random.key(seed), 10)
    grads = bell_draw(seeds[0], (TOKENS, D), 1.0, 6.0, ((0, 64), (1, 16)))
    routes_keys = jax.random.split(jax.random.fold_in(seeds[1], 1), TOKENS // TOK_DEV)
    routes_turns = jax.random.permutation(jax.random.fold_in(seeds[1], 3), TOKENS // TOK_DEV)
    routes = jax.vmap(lambda own, number: shared_out(jax.random.fold_in(seeds[1], 2), own, number, TOK_DEV, ALL_EXPERTS, 2, CAP, 2))(routes_keys, routes_turns).reshape((TOKENS, 2))
    gates = jnp.clip(0.2 + 0.8 * jax.random.uniform(seeds[2], (TOKENS, 2), jnp.float32) ** levels(seeds[2], (TOKENS, 2), ((0, 64),), -0.2, 0.2), 0.2, 1.0)
    dense_down = gaussian_with(seeds[3], (HID, D), HID ** -0.5, 0.15625, ((1, 16),), (1, 0, 16, 2.0))
    dense_up = bell_draw(seeds[4], (D, HID), D ** -0.5, 0.0625, ((0, 16),))
    dense_act = bell_draw(seeds[5], (TOKENS, HID), 1.5, 6.0, ((0, 64), (1, 16)))
    expert_down = gaussian_with(seeds[6], (2 * EXPERTS, HID // 2, D), HID ** -0.5, 0.15625, ((0, 64), (2, 16)), (2, 1, 16, 2.0))
    expert_up = bell_draw(seeds[7], (2 * EXPERTS, D, HID // 2), D ** -0.5, 0.0625, ((0, 64), (1, 16)))
    expert_act = bell_draw(seeds[8], (2 * EXPERTS, SLOTS, HID // 2), 1.5, 6.0, ((0, 64), (2, 16)))
    return {"grads": grads, "routes": routes, "gates": gates, "dense_down": dense_down, "dense_up": dense_up, "dense_act": dense_act, "expert_down": expert_down, "expert_up": expert_up, "expert_act": expert_act}


def slot_table(routes):
    route_grid = routes.reshape(-1, TOK_DEV * 2)
    onehot = (route_grid[:, :, None] == jnp.arange(ALL_EXPERTS, dtype=jnp.int32)[None, None, :]).astype(jnp.int32)
    earlier = jnp.cumsum(onehot, axis=1) - onehot
    return jnp.sum(earlier * onehot, axis=2).reshape(-1).astype(jnp.int32)


def blocked(left, right):
    block_width = D // N_TENSOR
    combined = jnp.zeros((left.shape[0], right.shape[0]), jnp.float32)
    for shard in range(N_TENSOR):
        lo_col = shard * block_width
        block_sum = jnp.dot(left[:, lo_col:lo_col + block_width], right[:, lo_col:lo_col + block_width].T, preferred_element_type=jnp.float32)
        block_sum = lax.optimization_barrier(block_sum.astype(jnp.bfloat16))
        combined = combined + block_sum.astype(jnp.float32)
    return combined


def reference(grads, routes, gates, dense_down, dense_up, dense_act, expert_down, expert_up, expert_act):
    route_ids = routes.reshape(-1).astype(jnp.int32)
    slot_rank = slot_table(routes)
    block_index = (jnp.arange(TOKENS * 2, dtype=jnp.int32) // (TOK_DEV * 2)).astype(jnp.int32)
    in_window = route_ids < EXPERTS
    target = jnp.where(in_window, route_ids * SLOTS + block_index * CAP + slot_rank, EXPERTS * SLOTS).astype(jnp.int32)
    routed = (grads.astype(jnp.float32)[:, None, :] * gates[:, :, None]).astype(jnp.bfloat16).reshape(-1, D)
    dispatched = jnp.zeros((EXPERTS * SLOTS + 1, D), jnp.bfloat16).at[target].set(routed)
    dispatched = dispatched[:-1].reshape(EXPERTS, SLOTS, D)
    dense_mid = blocked(grads, dense_down)
    dense_half = (dense_mid * jax.nn.silu(dense_act.astype(jnp.float32))).astype(jnp.bfloat16)
    dense_dx = jnp.dot(dense_half, dense_up.T, preferred_element_type=jnp.float32)
    half_width = HID // 2
    downs = expert_down.reshape(EXPERTS, 2, half_width, D)
    ups = expert_up.reshape(EXPERTS, 2, D, half_width)
    acts = expert_act.reshape(EXPERTS, 2, SLOTS, half_width)

    def per_expert(members):
        routed_rows, down_pair, up_pair, act_pair = members
        total = jnp.zeros((SLOTS, D), jnp.float32)
        for half in range(2):
            expert_mid = blocked(routed_rows, down_pair[half])
            expert_half = (expert_mid * jax.nn.silu(act_pair[half].astype(jnp.float32))).astype(jnp.bfloat16)
            part_dx = jnp.dot(expert_half, up_pair[half].T, preferred_element_type=jnp.float32).astype(jnp.bfloat16)
            total = total + part_dx.astype(jnp.float32)
        return total

    expert_dx = lax.map(per_expert, (dispatched, downs, ups, acts))
    flat_dx = jnp.concatenate([expert_dx.reshape(-1, D), jnp.zeros((1, D), jnp.float32)], axis=0)
    gathered_back = flat_dx[target].reshape(TOKENS, 2, D)
    return (dense_dx + jnp.sum(gathered_back, axis=1)).astype(jnp.bfloat16)
```

```python
import jax
import jax.numpy as jnp
from jax import lax
from jax.sharding import Mesh, PartitionSpec as P

CAP = 6
SWAP = [(0, 1), (1, 0)]


def contract_last(left, right):
    return lax.dot_general(
        left, right, (((1,), (1,)), ((), ())), preferred_element_type=jnp.float32
    )


def shards(
    grads, routes, gates, dense_down, dense_up, dense_act, expert_down, expert_up, expert_act
):
    held = lax.axis_size("z")
    parts = lax.axis_size("t")
    tokens, width = grads.shape
    half = expert_down.shape[1]
    piece = half // parts
    slots = held * CAP
    core = lax.axis_index("c")

    down_other = lax.ppermute(expert_down[0], "c", SWAP)
    up_other = lax.ppermute(expert_up[0], "c", SWAP)
    act_other = lax.ppermute(expert_act[0], "c", SWAP)

    ids = routes.T
    experts = jnp.arange(held, dtype=jnp.int32)[:, None]
    first, second = ids[0:1] == experts, ids[1:2] == experts
    named = (first | second).astype(jnp.bfloat16)
    before = (jnp.arange(tokens)[:, None] < jnp.arange(tokens)[None, :]).astype(jnp.bfloat16)
    rank = jnp.dot(named, before, preferred_element_type=jnp.float32).astype(jnp.int32)
    place = experts * CAP + rank + 1
    slot_ids = jnp.arange(slots, dtype=jnp.int32)[:, None]
    hit_first = (jnp.sum(jnp.where(first, place, 0), axis=0, keepdims=True) - 1) == slot_ids
    hit_second = (jnp.sum(jnp.where(second, place, 0), axis=0, keepdims=True) - 1) == slot_ids
    gate_rows = gates.T
    slot_gate = jnp.sum(
        jnp.where(hit_first, gate_rows[0:1], 0.0) + jnp.where(hit_second, gate_rows[1:2], 0.0),
        axis=1,
        keepdims=True,
    )
    chooser = (hit_first | hit_second).astype(jnp.bfloat16)
    outgoing = (
        jnp.dot(chooser, grads, preferred_element_type=jnp.float32) * slot_gate
    ).astype(jnp.bfloat16)
    arrived = lax.all_to_all(outgoing.reshape(held, CAP, width), "z", 0, 0, tiled=True).reshape(
        slots, width
    )

    def interleaved(own, other):
        return jnp.concatenate(
            [own.reshape(parts, piece, width), other.reshape(parts, piece, width)], axis=1
        ).reshape(2 * half, width)

    down_both = interleaved(expert_down[0], down_other)
    up_both = interleaved(expert_up[0].T, up_other.T)
    act_both = jnp.concatenate([expert_act[0].T, act_other.T], axis=0)
    act_rows = lax.dynamic_index_in_dim(
        act_both.reshape(2 * piece, held, 2, CAP), core, axis=2, keepdims=False
    ).reshape(2 * piece, slots)
    act = jnp.concatenate([act_rows, dense_act.T], axis=1).astype(jnp.float32)

    mid = jnp.concatenate(
        [contract_last(down_both, arrived), contract_last(dense_down, grads)], axis=1
    ).astype(jnp.bfloat16)
    shares = lax.all_to_all(
        mid.reshape(parts, 2 * piece, slots + tokens), "t", 0, 0, tiled=True
    )
    total = jnp.sum(shares.astype(jnp.float32), axis=0)
    hidden = (total * jax.nn.silu(act)).astype(jnp.bfloat16)
    full = lax.all_gather(hidden, "t", axis=0, tiled=True)

    rows = lax.dot_general(
        full[:, :slots], up_both, (((0,), (0,)), ((), ())), preferred_element_type=jnp.float32
    ).astype(jnp.bfloat16)
    returned = lax.all_to_all(rows.reshape(held, CAP, width), "z", 0, 0, tiled=True).reshape(
        slots, width
    )
    dense_sum = lax.dot_general(
        full[:, slots:], dense_up, (((0,), (1,)), ((), ())), preferred_element_type=jnp.float32
    )
    routed_back = lax.dot_general(
        chooser, returned, (((0,), (0,)), ((), ())), preferred_element_type=jnp.float32
    )
    return (dense_sum + routed_back).astype(jnp.bfloat16)


def solution(mesh):
    groups, parts = mesh.devices.shape
    split = Mesh(mesh.devices.reshape(groups // 2, 2, parts), ("z", "c", "t"))
    blocks = ("z", "c")
    placed = (
        P(blocks, "t"),
        P(blocks, None),
        P(blocks, None),
        P(None, "t"),
        P("t", None),
        P(blocks, "t"),
        P(blocks, None, "t"),
        P(blocks, "t", None),
        P(blocks, None, "t"),
    )
    return jax.shard_map(
        shards, mesh=split, in_specs=placed, out_specs=P(blocks, "t"), check_vma=False
    )
```

```python
import jax
import jax.numpy as jnp
from jax import lax
from jax.experimental import pallas as pl
from jax.experimental.pallas import tpu as pltpu
from jax.sharding import Mesh, PartitionSpec as P

CAP = 6
LANES = 128
F32 = jnp.float32
BF16 = jnp.bfloat16


def call(kernel, outs, *operands, flops=0):
    size = sum(v.size * v.dtype.itemsize for v in operands)
    return pl.pallas_call(
        kernel,
        out_shape=outs,
        compiler_params=pltpu.CompilerParams(vmem_limit_bytes=40 * 1024 * 1024),
        cost_estimate=pl.CostEstimate(flops=flops, bytes_accessed=size, transcendentals=0),
    )(*operands)


def dot(left, right, left_dim, right_dim):
    return lax.dot_general(
        left, right, (((left_dim,), (right_dim,)), ((), ())), preferred_element_type=F32
    )


def iota(shape, dim):
    return lax.broadcasted_iota(jnp.int32, shape, dim)


def packed(blocks, last):
    rows = last.shape[0]
    place = iota(last.shape, 0) & 7
    groups = [
        jnp.where(place >= CAP, pltpu.roll(last, CAP - 2 * j, 0), block).reshape(
            rows // 8, 8, LANES
        )
        for j, block in enumerate(blocks)
    ]
    return jnp.concatenate(groups, axis=1).astype(BF16)


def unpacked(message):
    wide = message.astype(F32)
    rows = wide.shape[0] * 8
    blocks = [wide[:, 8 * j : 8 * j + 8, :].reshape(rows, LANES) for j in range(3)]
    place = iota((rows, LANES), 0) & 7
    moved = [pltpu.roll(block, rows - CAP + 2 * j, 0) for j, block in enumerate(blocks)]
    last = jnp.where(place < 2, moved[0], jnp.where(place < 4, moved[1], moved[2]))
    last = jnp.where(iota((rows, LANES), 1) >= LANES // 2, last, 0.0)
    return [v.astype(BF16) for v in blocks + [last]]


def dispatch_kernel(routes, gates, grads_t, message, chooser):
    held = message.shape[0]
    tokens = routes.shape[1]
    ids = routes[...]
    experts = iota((held, tokens), 0)
    first, second = ids[0:1] == experts, ids[1:2] == experts
    named = jnp.where(first | second, 1.0, 0.0).astype(BF16)
    before = jnp.where(
        iota((tokens, tokens), 0) < iota((tokens, tokens), 1), 1.0, 0.0
    ).astype(BF16)
    place = experts * 8 + dot(named, before, 1, 0).astype(jnp.int32) + 1
    row = iota((held * 8, tokens), 0) + 1
    hit_first = jnp.sum(jnp.where(first, place, 0), axis=0, keepdims=True) == row
    hit_second = jnp.sum(jnp.where(second, place, 0), axis=0, keepdims=True) == row
    weight = gates[...]
    gate = jnp.sum(
        jnp.where(hit_first, weight[0:1], 0.0) + jnp.where(hit_second, weight[1:2], 0.0),
        axis=1,
        keepdims=True,
    )
    chosen = jnp.where(hit_first | hit_second, 1.0, 0.0).astype(BF16)
    chooser[...] = chosen
    width = grads_t.shape[0]
    rows = dot(chosen, grads_t[...], 1, 1)
    tail = dot(chosen, grads_t[width - LANES :, :], 1, 1) * gate
    message[...] = packed(
        [rows[:, LANES * j : LANES * (j + 1)] * gate for j in range(3)], tail
    )


def down_kernel(arrived, down_t, mid):
    cores, held = arrived.shape[0], arrived.shape[1]
    blocks = unpacked(arrived[...].reshape(cores * held, 3 * 8, LANES))
    slots, rows = cores * held * CAP, cores * held * 8
    row = iota((slots, rows), 1)
    core = jnp.where(row >= held * 8, 1, 0)
    block = ((row - core * held * 8) >> 3) * 2 + core
    pick = ((row & 7) < CAP) & (block * CAP + (row & 7) == iota((slots, rows), 0))
    pick = jnp.where(pick, 1.0, 0.0).astype(BF16)
    picked = dot(pick, jnp.concatenate(blocks, axis=1), 1, 0).astype(BF16)
    width = down_t.shape[0]
    weights = jnp.concatenate([down_t[: 3 * LANES, :], down_t[width - LANES :, :]], axis=0)
    total = dot(weights, picked, 0, 1)
    piece = mid.shape[1]
    for part in range(mid.shape[0]):
        mid[part] = total[piece * part : piece * (part + 1)].astype(BF16)


def gate_kernel(shares, act, copies):
    total = shares[0].astype(F32)
    for part in range(1, shares.shape[0]):
        total = total + shares[part].astype(F32)
    value = act[...].astype(F32)
    hidden = (total * (value / (1.0 + jnp.exp(-value)))).astype(BF16)
    for part in range(copies.shape[0]):
        copies[part] = hidden


def up_kernel(full, up, rows_t, stacked):
    piece = full.shape[1]
    for part in range(full.shape[0]):
        stacked[piece * part : piece * (part + 1), :] = full[part].astype(F32)
    rows_t[...] = dot(up[...], stacked[...].astype(BF16), 1, 0).astype(BF16)


def return_kernel(core_id, halves, message):
    held = message.shape[0]
    slots = halves.shape[2]
    core = core_id[0]
    both = (halves[0].astype(F32) + halves[1].astype(F32)).astype(BF16)
    row = iota((held * 8, slots), 0)
    slot = ((row >> 3) * 2 + core) * CAP + (row & 7)
    pick = ((row & 7) < CAP) & (slot == iota((held * 8, slots), 1))
    pick = jnp.where(pick, 1.0, 0.0).astype(BF16)
    width = both.shape[0]
    rows = dot(pick, both, 1, 1)
    message[...] = packed(
        [rows[:, LANES * j : LANES * (j + 1)] for j in range(3)],
        dot(pick, both[width - LANES :], 1, 1),
    )


def combine_kernel(returned, chooser, dense_t, out_t):
    blocks = unpacked(returned[...])
    chosen = chooser[...]
    width = out_t.shape[0]
    for j in range(3):
        low = LANES * j
        out_t[low : low + LANES, :] = (
            dense_t[low : low + LANES, :] + dot(blocks[j], chosen, 0, 0)
        ).astype(BF16)
    half = LANES // 2
    out_t[3 * LANES :, :] = (
        dense_t[3 * LANES :, :] + dot(blocks[3], chosen, 0, 0)[half:]
    ).astype(BF16)


def turn(axis, step):
    size = lax.axis_size(axis)
    return [(i, (i + step) % size) for i in range(size)]


def scattered(blocks, axis):
    size, me = lax.axis_size(axis), lax.axis_index(axis)
    total = lax.dynamic_index_in_dim(blocks, me, 0, keepdims=False).astype(F32)
    for step in range(1, size):
        block = lax.dynamic_index_in_dim(blocks, (me + step) % size, 0, keepdims=False)
        total = total + lax.ppermute(block, axis, turn(axis, step)).astype(F32)
    return total


def gathered(block, axis):
    size, me = lax.axis_size(axis), lax.axis_index(axis)
    out = jnp.zeros((size,) + block.shape, block.dtype)
    for step in range(size):
        piece = lax.ppermute(block, axis, turn(axis, step)) if step else block
        out = lax.dynamic_update_index_in_dim(out, piece, (me - step) % size, 0)
    return out


def shards(
    grads, routes, gates, dense_down, dense_up, dense_act, expert_down, expert_up, expert_act
):
    held = lax.axis_size("z")
    across, along = lax.axis_size("x"), lax.axis_size("y")
    parts = across * along
    tokens, width = grads.shape
    half = expert_down.shape[1]
    piece, share = half // parts, dense_act.shape[1]
    slots = expert_act.shape[1]
    tensor = ("x", "y")

    message, chooser = call(
        dispatch_kernel,
        (
            jax.ShapeDtypeStruct((held, 24, LANES), BF16),
            jax.ShapeDtypeStruct((held * 8, tokens), BF16),
        ),
        routes.T,
        gates.T,
        grads.T,
    )
    arrived = lax.all_to_all(message, "z", 0, 0, tiled=True)

    dense_mid = dot(dense_down, grads, 1, 1).astype(BF16)
    dense_mid = dense_mid.reshape(across, along, share, tokens)
    dense_share = scattered(scattered(dense_mid, "x").astype(BF16), "y")

    mid = call(
        down_kernel,
        jax.ShapeDtypeStruct((parts, piece, slots), BF16),
        lax.all_gather(arrived, "c", axis=0, tiled=False),
        expert_down[0].T,
    )
    shares = lax.all_to_all(mid, tensor, 0, 0, tiled=True)
    copies = call(
        gate_kernel,
        jax.ShapeDtypeStruct((parts, piece, slots), BF16),
        shares,
        expert_act[0].T,
    )
    full = lax.all_to_all(copies, tensor, 0, 0, tiled=True)
    size = full.size * 2 + expert_up.size * 2
    rows_t = pl.pallas_call(
        up_kernel,
        out_shape=jax.ShapeDtypeStruct((width, slots), BF16),
        scratch_shapes=[pltpu.VMEM((half, slots), F32)],
        compiler_params=pltpu.CompilerParams(vmem_limit_bytes=40 * 1024 * 1024),
        cost_estimate=pl.CostEstimate(flops=0, bytes_accessed=size, transcendentals=0),
    )(full, expert_up[0])
    back = pl.pallas_call(
        return_kernel,
        out_shape=jax.ShapeDtypeStruct((held, 24, LANES), BF16),
        in_specs=[
            pl.BlockSpec(memory_space=pltpu.SMEM),
            pl.BlockSpec(memory_space=pltpu.VMEM),
        ],
        compiler_params=pltpu.CompilerParams(vmem_limit_bytes=40 * 1024 * 1024),
    )(
        lax.axis_index("c").astype(jnp.int32).reshape(1),
        lax.all_gather(rows_t, "c", axis=0, tiled=False),
    )
    returned = lax.all_to_all(back, "z", 0, 0, tiled=True)

    value = dense_act.T.astype(F32)
    dense_hidden = (dense_share * jax.nn.silu(value)).astype(BF16)
    dense_full = gathered(gathered(dense_hidden, "y"), "x").reshape(parts * share, tokens)
    dense_t = dot(dense_up, dense_full, 1, 0)
    out_t = call(
        combine_kernel, jax.ShapeDtypeStruct((width, tokens), BF16), returned, chooser, dense_t
    )
    return out_t.T


def solution(mesh):
    groups, parts = mesh.devices.shape
    across = 4 if parts == 16 else 2
    split = Mesh(
        mesh.devices.reshape(groups // 2, 2, across, parts // across), ("z", "c", "x", "y")
    )
    blocks, tensor = ("z", "c"), ("x", "y")
    placed = (
        P(blocks, tensor),
        P(blocks, None),
        P(blocks, None),
        P(None, tensor),
        P(tensor, None),
        P(blocks, tensor),
        P(blocks, None, tensor),
        P(blocks, tensor, None),
        P(blocks, None, tensor),
    )
    return jax.shard_map(
        shards, mesh=split, in_specs=placed, out_specs=P(blocks, tensor), check_vma=False
    )
```

```python
import jax
import jax.numpy as jnp
from jax import lax
from jax.experimental import pallas as pl
from jax.experimental.pallas import tpu as pltpu
from jax.sharding import Mesh, PartitionSpec as P

CAP = 6
LANES = 128
ROOM = 60
F32 = jnp.float32
BF16 = jnp.bfloat16


def call(kernel, outs, *operands, room=40):
    size = sum(v.size * v.dtype.itemsize for v in operands)
    return pl.pallas_call(
        kernel,
        out_shape=outs,
        compiler_params=pltpu.CompilerParams(vmem_limit_bytes=room * 1024 * 1024),
        cost_estimate=pl.CostEstimate(flops=0, bytes_accessed=size, transcendentals=0),
    )(*operands)


def dot(left, right, left_dim, right_dim):
    return lax.dot_general(
        left, right, (((left_dim,), (right_dim,)), ((), ())), preferred_element_type=F32
    )


def iota(shape, dim):
    return lax.broadcasted_iota(jnp.int32, shape, dim)


def packed(blocks, last):
    rows = last.shape[0]
    place = iota(last.shape, 0) & 7
    groups = [
        jnp.where(place >= CAP, pltpu.roll(last, CAP - 2 * j, 0), block).reshape(
            rows // 8, 8, LANES
        )
        for j, block in enumerate(blocks)
    ]
    return jnp.concatenate(groups, axis=1).astype(BF16)


def unpacked(message):
    wide = message.astype(F32)
    rows = wide.shape[0] * 8
    blocks = [wide[:, 8 * j : 8 * j + 8, :].reshape(rows, LANES) for j in range(3)]
    place = iota((rows, LANES), 0) & 7
    moved = [pltpu.roll(block, rows - CAP + 2 * j, 0) for j, block in enumerate(blocks)]
    last = jnp.where(place < 2, moved[0], jnp.where(place < 4, moved[1], moved[2]))
    last = jnp.where(iota((rows, LANES), 1) >= LANES // 2, last, 0.0)
    return [v.astype(BF16) for v in blocks + [last]]


def dispatch_kernel(routes, gates, grads_t, message, chooser):
    held = message.shape[0]
    tokens = routes.shape[1]
    ids = routes[...]
    experts = iota((held, tokens), 0)
    first, second = ids[0:1] == experts, ids[1:2] == experts
    named = jnp.where(first | second, 1.0, 0.0).astype(BF16)
    before = jnp.where(
        iota((tokens, tokens), 0) < iota((tokens, tokens), 1), 1.0, 0.0
    ).astype(BF16)
    place = experts * 8 + dot(named, before, 1, 0).astype(jnp.int32) + 1
    row = iota((held * 8, tokens), 0) + 1
    hit_first = jnp.sum(jnp.where(first, place, 0), axis=0, keepdims=True) == row
    hit_second = jnp.sum(jnp.where(second, place, 0), axis=0, keepdims=True) == row
    weight = gates[...]
    gate = jnp.sum(
        jnp.where(hit_first, weight[0:1], 0.0) + jnp.where(hit_second, weight[1:2], 0.0),
        axis=1,
        keepdims=True,
    )
    chosen = jnp.where(hit_first | hit_second, 1.0, 0.0).astype(BF16)
    chooser[...] = chosen
    width = grads_t.shape[0]
    rows = dot(chosen, grads_t[...], 1, 1)
    tail = dot(chosen, grads_t[width - LANES :, :], 1, 1) * gate
    message[...] = packed(
        [rows[:, LANES * j : LANES * (j + 1)] * gate for j in range(3)], tail
    )


def down_kernel(arrived, down_t, mid):
    cores, held = arrived.shape[0], arrived.shape[1]
    blocks = unpacked(arrived[...].reshape(cores * held, 3 * 8, LANES))
    slots, rows = cores * held * CAP, cores * held * 8
    row = iota((slots, rows), 1)
    core = jnp.where(row >= held * 8, 1, 0)
    block = ((row - core * held * 8) >> 3) * 2 + core
    pick = ((row & 7) < CAP) & (block * CAP + (row & 7) == iota((slots, rows), 0))
    pick = jnp.where(pick, 1.0, 0.0).astype(BF16)
    picked = dot(pick, jnp.concatenate(blocks, axis=1), 1, 0).astype(BF16)
    width = down_t.shape[0]
    weights = jnp.concatenate([down_t[: 3 * LANES, :], down_t[width - LANES :, :]], axis=0)
    total = dot(weights, picked, 0, 1)
    piece = mid.shape[1]
    for part in range(mid.shape[0]):
        mid[part] = total[piece * part : piece * (part + 1)].astype(BF16)


def gate_kernel(shares, act, copies):
    total = shares[0].astype(F32)
    for part in range(1, shares.shape[0]):
        total = total + shares[part].astype(F32)
    value = act[...].astype(F32)
    hidden = (total * (value / (1.0 + jnp.exp(-value)))).astype(BF16)
    for part in range(copies.shape[0]):
        copies[part] = hidden


def up_kernel(full, up, rows_t, stacked):
    piece = full.shape[1]
    for part in range(full.shape[0]):
        stacked[piece * part : piece * (part + 1), :] = full[part].astype(F32)
    rows_t[...] = dot(up[...], stacked[...].astype(BF16), 1, 0).astype(BF16)


def return_kernel(core_id, halves, message):
    held = message.shape[0]
    slots = halves.shape[2]
    core = core_id[0]
    both = (halves[0].astype(F32) + halves[1].astype(F32)).astype(BF16)
    row = iota((held * 8, slots), 0)
    slot = ((row >> 3) * 2 + core) * CAP + (row & 7)
    pick = ((row & 7) < CAP) & (slot == iota((held * 8, slots), 1))
    pick = jnp.where(pick, 1.0, 0.0).astype(BF16)
    width = both.shape[0]
    rows = dot(pick, both, 1, 1)
    message[...] = packed(
        [rows[:, LANES * j : LANES * (j + 1)] for j in range(3)],
        dot(pick, both[width - LANES :], 1, 1),
    )


def combine_kernel(returned, chooser, dense_t, out_t):
    blocks = unpacked(returned[...])
    chosen = chooser[...]
    width = out_t.shape[0]
    for j in range(3):
        low = LANES * j
        out_t[low : low + LANES, :] = (
            dense_t[low : low + LANES, :] + dot(blocks[j], chosen, 0, 0)
        ).astype(BF16)
    half = LANES // 2
    out_t[3 * LANES :, :] = (
        dense_t[3 * LANES :, :] + dot(blocks[3], chosen, 0, 0)[half:]
    ).astype(BF16)


def turn(axis, step):
    size = lax.axis_size(axis)
    return [(i, (i + step) % size) for i in range(size)]


def scattered(blocks, axis):
    size, me = lax.axis_size(axis), lax.axis_index(axis)
    total = lax.dynamic_index_in_dim(blocks, me, 0, keepdims=False).astype(F32)
    for step in range(1, size):
        block = lax.dynamic_index_in_dim(blocks, (me + step) % size, 0, keepdims=False)
        total = total + lax.ppermute(block, axis, turn(axis, step)).astype(F32)
    return total


def gathered(block, axis):
    size, me = lax.axis_size(axis), lax.axis_index(axis)
    out = jnp.zeros((size,) + block.shape, block.dtype)
    for step in range(size):
        piece = lax.ppermute(block, axis, turn(axis, step)) if step else block
        out = lax.dynamic_update_index_in_dim(out, piece, (me - step) % size, 0)
    return out


def shards(
    grads, routes, gates, dense_down, dense_up, dense_act, expert_down, expert_up, expert_act
):
    held = lax.axis_size("z")
    across, along = lax.axis_size("x"), lax.axis_size("y")
    parts = across * along
    tokens, width = grads.shape
    half = expert_down.shape[1]
    piece, share = half // parts, dense_act.shape[1]
    slots = expert_act.shape[1]
    tensor = ("x", "y")

    message, chooser = call(
        dispatch_kernel,
        (
            jax.ShapeDtypeStruct((held, 24, LANES), BF16),
            jax.ShapeDtypeStruct((held * 8, tokens), BF16),
        ),
        routes.T,
        gates.T,
        grads.T,
        room=ROOM,
    )
    message, dense_rows = lax.optimization_barrier((message, grads.T))
    arrived = lax.all_to_all(message, "z", 0, 0, tiled=True)
    dense_mid = dot(dense_down, dense_rows, 1, 0).astype(BF16)
    dense_mid = dense_mid.reshape(across, along, share, tokens)
    dense_sum = scattered(dense_mid, "x").astype(BF16)
    arrived, dense_sum = lax.optimization_barrier((arrived, dense_sum))

    mid = call(
        down_kernel,
        jax.ShapeDtypeStruct((parts, piece, slots), BF16),
        lax.all_gather(arrived, "c", axis=0, tiled=False),
        expert_down[0].T,
        room=ROOM,
    )
    mid, dense_sum = lax.optimization_barrier((mid, dense_sum))
    shares = lax.all_to_all(mid, tensor, 0, 0, tiled=True)
    dense_share = scattered(dense_sum, "y")
    shares, dense_share = lax.optimization_barrier((shares, dense_share))
    copies = call(
        gate_kernel,
        jax.ShapeDtypeStruct((parts, piece, slots), BF16),
        shares,
        expert_act[0].T,
    )
    copies, dense_share = lax.optimization_barrier((copies, dense_share))
    full = lax.all_to_all(copies, tensor, 0, 0, tiled=True)
    dense_hidden = (dense_share * jax.nn.silu(dense_act.T.astype(F32))).astype(BF16)
    dense_column = gathered(dense_hidden, "y")
    full, dense_column = lax.optimization_barrier((full, dense_column))
    size = full.size * 2 + expert_up.size * 2
    rows_t = pl.pallas_call(
        up_kernel,
        out_shape=jax.ShapeDtypeStruct((width, slots), BF16),
        scratch_shapes=[pltpu.VMEM((half, slots), F32)],
        compiler_params=pltpu.CompilerParams(vmem_limit_bytes=40 * 1024 * 1024),
        cost_estimate=pl.CostEstimate(flops=0, bytes_accessed=size, transcendentals=0),
    )(full, expert_up[0])
    back = pl.pallas_call(
        return_kernel,
        out_shape=jax.ShapeDtypeStruct((held, 24, LANES), BF16),
        in_specs=[
            pl.BlockSpec(memory_space=pltpu.SMEM),
            pl.BlockSpec(memory_space=pltpu.VMEM),
        ],
        compiler_params=pltpu.CompilerParams(vmem_limit_bytes=40 * 1024 * 1024),
    )(
        lax.axis_index("c").astype(jnp.int32).reshape(1),
        lax.all_gather(rows_t, "c", axis=0, tiled=False),
    )
    back, dense_column = lax.optimization_barrier((back, dense_column))
    returned = lax.all_to_all(back, "z", 0, 0, tiled=True)
    dense_full = gathered(dense_column, "x").reshape(parts * share, tokens)
    dense_t = dot(dense_up, dense_full, 1, 0)
    out_t = call(
        combine_kernel, jax.ShapeDtypeStruct((width, tokens), BF16), returned, chooser, dense_t
    )
    return out_t.T


def solution(mesh):
    groups, parts = mesh.devices.shape
    across = 4 if parts == 16 else 2
    split = Mesh(
        mesh.devices.reshape(groups // 2, 2, across, parts // across), ("z", "c", "x", "y")
    )
    blocks, tensor = ("z", "c"), ("x", "y")
    placed = (
        P(blocks, tensor),
        P(blocks, None),
        P(blocks, None),
        P(None, tensor),
        P(tensor, None),
        P(blocks, tensor),
        P(blocks, None, tensor),
        P(blocks, tensor, None),
        P(blocks, None, tensor),
    )
    return jax.shard_map(
        shards, mesh=split, in_specs=placed, out_specs=P(blocks, tensor), check_vma=False
    )
```

```python
import jax
import jax.numpy as jnp
from jax import lax
from jax.experimental import pallas as pl
from jax.experimental.pallas import tpu as pltpu
from jax.sharding import Mesh, PartitionSpec as P

CAP = 6
LANES = 128
ROOM = 60
F32 = jnp.float32
BF16 = jnp.bfloat16


def call(kernel, outs, *operands, room=20, scratch=(), spaces=None, out_space=pltpu.VMEM):
    size = sum(v.size * v.dtype.itemsize for v in operands)
    spaces = spaces or [pltpu.VMEM] * len(operands)
    return pl.pallas_call(
        kernel,
        out_shape=outs,
        in_specs=[pl.BlockSpec(memory_space=space) for space in spaces],
        out_specs=jax.tree.map(lambda _: pl.BlockSpec(memory_space=out_space), outs),
        scratch_shapes=list(scratch),
        compiler_params=pltpu.CompilerParams(vmem_limit_bytes=room * 1024 * 1024),
        cost_estimate=pl.CostEstimate(flops=0, bytes_accessed=size, transcendentals=0),
    )(*operands)


def dot(left, right, left_dim, right_dim):
    return lax.dot_general(
        left, right, (((left_dim,), (right_dim,)), ((), ())), preferred_element_type=F32
    )


def iota(shape, dim):
    return lax.broadcasted_iota(jnp.int32, shape, dim)


def packed(blocks, last):
    rows = last.shape[0]
    place = iota(last.shape, 0) & 7
    groups = [
        jnp.where(place >= CAP, pltpu.roll(last, CAP - 2 * j, 0), block).reshape(
            rows // 8, 8, LANES
        )
        for j, block in enumerate(blocks)
    ]
    return jnp.concatenate(groups, axis=1).astype(BF16)


def unpacked(message):
    wide = message.astype(F32)
    rows = wide.shape[0] * 8
    blocks = [wide[:, 8 * j : 8 * j + 8, :].reshape(rows, LANES) for j in range(3)]
    place = iota((rows, LANES), 0) & 7
    moved = [pltpu.roll(block, rows - CAP + 2 * j, 0) for j, block in enumerate(blocks)]
    last = jnp.where(place < 2, moved[0], jnp.where(place < 4, moved[1], moved[2]))
    last = jnp.where(iota((rows, LANES), 1) >= LANES // 2, last, 0.0)
    return [v.astype(BF16) for v in blocks + [last]]


def dispatch_kernel(routes, gates, grads_t, message, chooser):
    held = message.shape[0]
    tokens = routes.shape[1]
    ids = routes[...]
    experts = iota((held, tokens), 0)
    first, second = ids[0:1] == experts, ids[1:2] == experts
    named = jnp.where(first | second, 1.0, 0.0).astype(BF16)
    before = jnp.where(
        iota((tokens, tokens), 0) < iota((tokens, tokens), 1), 1.0, 0.0
    ).astype(BF16)
    place = experts * 8 + dot(named, before, 1, 0).astype(jnp.int32) + 1
    row = iota((held * 8, tokens), 0) + 1
    hit_first = jnp.sum(jnp.where(first, place, 0), axis=0, keepdims=True) == row
    hit_second = jnp.sum(jnp.where(second, place, 0), axis=0, keepdims=True) == row
    weight = gates[...]
    gate = jnp.sum(
        jnp.where(hit_first, weight[0:1], 0.0) + jnp.where(hit_second, weight[1:2], 0.0),
        axis=1,
        keepdims=True,
    )
    chosen = jnp.where(hit_first | hit_second, 1.0, 0.0).astype(BF16)
    chooser[...] = chosen
    width = grads_t.shape[0]
    rows = dot(chosen, grads_t[...], 1, 1)
    tail = dot(chosen, grads_t[width - LANES :, :], 1, 1) * gate
    message[...] = packed(
        [rows[:, LANES * j : LANES * (j + 1)] * gate for j in range(3)], tail
    )


def down_kernel(arrived, down_t, mid, held_out, sems):
    cores, held = arrived.shape[0], arrived.shape[1]
    blocks = unpacked(arrived[...].reshape(cores * held, 3 * 8, LANES))
    slots, rows = cores * held * CAP, cores * held * 8
    row = iota((slots, rows), 1)
    core = jnp.where(row >= held * 8, 1, 0)
    block = ((row - core * held * 8) >> 3) * 2 + core
    pick = ((row & 7) < CAP) & (block * CAP + (row & 7) == iota((slots, rows), 0))
    pick = jnp.where(pick, 1.0, 0.0).astype(BF16)
    picked = dot(pick, jnp.concatenate(blocks, axis=1), 1, 0).astype(BF16)
    width = down_t.shape[0]
    weights = jnp.concatenate([down_t[: 3 * LANES, :], down_t[width - LANES :, :]], axis=0)
    total = dot(weights, picked, 0, 1)
    piece = mid.shape[1]
    copies = []
    for part in range(mid.shape[0]):
        held_out[part] = total[piece * part : piece * (part + 1)].astype(BF16)
        copies.append(pltpu.make_async_copy(held_out.at[part], mid.at[part], sems.at[part]))
        copies[part].start()
    for copy in copies:
        copy.wait()


def gate_kernel(shares, act, copies, held_out, sems):
    total = shares[0].astype(F32)
    for part in range(1, shares.shape[0]):
        total = total + shares[part].astype(F32)
    value = act[...].astype(F32)
    held_out[...] = (total * (value / (1.0 + jnp.exp(-value)))).astype(BF16)
    sent = [
        pltpu.make_async_copy(held_out, copies.at[part], sems.at[part])
        for part in range(copies.shape[0])
    ]
    for copy in sent:
        copy.start()
    for copy in sent:
        copy.wait()


def hold_kernel(weights, held_in, sem):
    copy = pltpu.make_async_copy(weights, held_in, sem)
    copy.start()
    copy.wait()


def up_kernel(full, up, rows_t, stacked):
    piece = full.shape[1]
    for part in range(full.shape[0]):
        stacked[piece * part : piece * (part + 1), :] = full[part].astype(F32)
    rows_t[...] = dot(up[...], stacked[...].astype(BF16), 1, 0).astype(BF16)


def return_kernel(core_id, halves, message):
    held = message.shape[0]
    slots = halves.shape[2]
    core = core_id[0]
    both = (halves[0].astype(F32) + halves[1].astype(F32)).astype(BF16)
    row = iota((held * 8, slots), 0)
    slot = ((row >> 3) * 2 + core) * CAP + (row & 7)
    pick = ((row & 7) < CAP) & (slot == iota((held * 8, slots), 1))
    pick = jnp.where(pick, 1.0, 0.0).astype(BF16)
    width = both.shape[0]
    rows = dot(pick, both, 1, 1)
    message[...] = packed(
        [rows[:, LANES * j : LANES * (j + 1)] for j in range(3)],
        dot(pick, both[width - LANES :], 1, 1),
    )


def combine_kernel(returned, chooser, dense_t, out_t):
    blocks = unpacked(returned[...])
    chosen = chooser[...]
    width = out_t.shape[0]
    for j in range(3):
        low = LANES * j
        out_t[low : low + LANES, :] = (
            dense_t[low : low + LANES, :] + dot(blocks[j], chosen, 0, 0)
        ).astype(BF16)
    half = LANES // 2
    out_t[3 * LANES :, :] = (
        dense_t[3 * LANES :, :] + dot(blocks[3], chosen, 0, 0)[half:]
    ).astype(BF16)


def wrapped(value, size):
    value = jnp.where(value >= size, value - size, value)
    return jnp.where(value < 0, value + size, value)


def dense_down_kernel(place, down_t, grads_t, *rest):
    slabs, blocks = rest[:-1], rest[-1]
    size = len(slabs)
    blocks[...] = dot(down_t[...], grads_t[...], 0, 0).reshape(blocks.shape)
    for step in range(size):
        first = wrapped(place[0] + step, size) * place[2]
        for second in range(size):
            slabs[step][second] = blocks[first + second * place[3]].astype(BF16)


def dense_sum_kernel(place, *rest):
    size = len(rest) // 2
    slabs, sums = rest[:size], rest[size:]
    for step in range(size):
        second = wrapped(place[1] + step, size)
        total = slabs[0][second].astype(F32)
        for slab in slabs[1:]:
            total = total + slab[second].astype(F32)
        sums[step][...] = total.astype(sums[step].dtype)


def dense_gate_kernel(*rest):
    pieces, act, hidden = rest[:-2], rest[-2], rest[-1]
    total = pieces[0][...].astype(F32)
    for piece in pieces[1:]:
        total = total + piece[...].astype(F32)
    value = act[...].astype(F32)
    hidden[...] = (total * (value / (1.0 + jnp.exp(-value)))).astype(BF16)


def dense_up_kernel(place, *rest):
    slabs, up, out_t, blocks = rest[:-3], rest[-3], rest[-2], rest[-1]
    size = len(slabs)
    for back in range(size):
        first = wrapped(place[0] - back, size) * place[2]
        for step in range(size):
            second = wrapped(place[1] - step, size) * place[3]
            blocks[first + second] = slabs[back][step].astype(F32)
    full = blocks[...].reshape(up.shape[1], blocks.shape[2]).astype(BF16)
    out_t[...] = dot(up[...], full, 1, 0)


def moved(value, stage, step, size):
    pairs = []
    for core in range(2):
        for x in range(size):
            for y in range(size):
                if core == stage:
                    target = ((x + step) % size, y)
                else:
                    target = (x, (y + step) % size)
                pairs.append(
                    ((core * size + x) * size + y, (core * size + target[0]) * size + target[1])
                )
    return lax.ppermute(value, ("c", "x", "y"), pairs)


def shards(
    grads, routes, gates, dense_down, dense_up, dense_act, expert_down, expert_up, expert_act
):
    held = lax.axis_size("z")
    across, along = lax.axis_size("x"), lax.axis_size("y")
    parts = across * along
    tokens, width = grads.shape
    half = expert_down.shape[1]
    piece, share = half // parts, dense_act.shape[1]
    slots = expert_act.shape[1]
    tensor = ("x", "y")

    message, chooser = call(
        dispatch_kernel,
        (
            jax.ShapeDtypeStruct((held, 24, LANES), BF16),
            jax.ShapeDtypeStruct((held * 8, tokens), BF16),
        ),
        routes.T,
        gates.T,
        grads.T,
        room=ROOM,
    )
    core, x, y = lax.axis_index("c"), lax.axis_index("x"), lax.axis_index("y")
    place = jnp.stack(
        [
            jnp.where(core == 0, x, y),
            jnp.where(core == 0, y, x),
            jnp.where(core == 0, along, 1),
            jnp.where(core == 0, 1, along),
        ]
    ).astype(jnp.int32)
    smem, vmem = pltpu.SMEM, pltpu.VMEM
    slab = jax.ShapeDtypeStruct((along, share, tokens), BF16)
    piece_f32 = jax.ShapeDtypeStruct((share, tokens), F32)
    piece_bf16 = jax.ShapeDtypeStruct((share, tokens), BF16)
    blocks = pltpu.VMEM((parts, share, tokens), F32)
    steps = range(1, along)

    message, dense_rows = lax.optimization_barrier((message, grads.T))
    arrived = lax.all_to_all(message, "z", 0, 0, tiled=True)
    slabs = call(
        dense_down_kernel,
        (slab,) * along,
        place,
        dense_down.T,
        dense_rows,
        scratch=[blocks],
        spaces=[smem, vmem, vmem],
    )
    sums = call(
        dense_sum_kernel,
        (piece_f32,) + (piece_bf16,) * (along - 1),
        place,
        slabs[0],
        *[moved(slabs[step], 0, step, along) for step in steps],
        spaces=[smem] + [vmem] * along,
    )
    arrived, sums = lax.optimization_barrier((arrived, sums))

    parts_out = jax.ShapeDtypeStruct((parts, piece, slots), BF16)
    mid = call(
        down_kernel,
        parts_out,
        lax.all_gather(arrived, "c", axis=0, tiled=False),
        expert_down[0].T,
        scratch=[pltpu.VMEM((parts, piece, slots), BF16), pltpu.SemaphoreType.DMA((parts,))],
        out_space=pltpu.HBM,
    )
    mid, sums, up = lax.optimization_barrier((mid, sums, expert_up[0]))
    shares = lax.all_to_all(mid, tensor, 0, 0, tiled=True)
    pieces = [sums[0]] + [moved(sums[step], 1, step, along) for step in steps]
    up = call(
        hold_kernel,
        jax.ShapeDtypeStruct((width, half), BF16),
        up,
        scratch=[pltpu.SemaphoreType.DMA],
        spaces=[pltpu.HBM],
    )
    shares, pieces, up = lax.optimization_barrier((shares, pieces, up))
    copies = call(
        gate_kernel,
        parts_out,
        shares,
        expert_act[0].T,
        scratch=[pltpu.VMEM((piece, slots), BF16), pltpu.SemaphoreType.DMA((parts,))],
        out_space=pltpu.HBM,
    )
    copies, pieces = lax.optimization_barrier((copies, pieces))
    full = lax.all_to_all(copies, tensor, 0, 0, tiled=True)
    hidden = call(dense_gate_kernel, piece_bf16, *pieces, dense_act.T)
    columns = [hidden] + [moved(hidden, 1, step, along) for step in steps]
    full, columns = lax.optimization_barrier((full, columns))
    rows_t = call(
        up_kernel,
        jax.ShapeDtypeStruct((width, slots), BF16),
        full,
        up,
        scratch=[pltpu.VMEM((half, slots), F32)],
    )
    back = call(
        return_kernel,
        jax.ShapeDtypeStruct((held, 24, LANES), BF16),
        core.astype(jnp.int32).reshape(1),
        lax.all_gather(rows_t, "c", axis=0, tiled=False),
        spaces=[smem, vmem],
    )
    back, columns = lax.optimization_barrier((back, columns))
    returned = lax.all_to_all(back, "z", 0, 0, tiled=True)
    column = jnp.stack(columns)
    dense_t = call(
        dense_up_kernel,
        jax.ShapeDtypeStruct((width, tokens), F32),
        place,
        column,
        *[moved(column, 0, step, along) for step in steps],
        dense_up,
        scratch=[blocks],
        spaces=[smem] + [vmem] * (along + 1),
    )
    out_t = call(
        combine_kernel, jax.ShapeDtypeStruct((width, tokens), BF16), returned, chooser, dense_t
    )
    return out_t.T


def solution(mesh):
    groups, parts = mesh.devices.shape
    across = 4 if parts == 16 else 2
    split = Mesh(
        mesh.devices.reshape(groups // 2, 2, across, parts // across), ("z", "c", "x", "y")
    )
    blocks, tensor = ("z", "c"), ("x", "y")
    placed = (
        P(blocks, tensor),
        P(blocks, None),
        P(blocks, None),
        P(None, tensor),
        P(tensor, None),
        P(blocks, tensor),
        P(blocks, None, tensor),
        P(blocks, tensor, None),
        P(blocks, None, tensor),
    )
    return jax.shard_map(
        shards, mesh=split, in_specs=placed, out_specs=P(blocks, tensor), check_vma=False
    )
```

```python
import jax
import jax.numpy as jnp
from jax import lax
from jax.experimental import pallas as pl
from jax.experimental.pallas import tpu as pltpu
from jax.sharding import Mesh, PartitionSpec as P

CAP = 6
LANES = 128
ROOM = 60
F32 = jnp.float32
BF16 = jnp.bfloat16


def call(kernel, outs, *operands, room=20, scratch=(), spaces=None, out_space=pltpu.VMEM):
    size = sum(v.size * v.dtype.itemsize for v in operands)
    spaces = spaces or [pltpu.VMEM] * len(operands)
    return pl.pallas_call(
        kernel,
        out_shape=outs,
        in_specs=[pl.BlockSpec(memory_space=space) for space in spaces],
        out_specs=jax.tree.map(lambda _: pl.BlockSpec(memory_space=out_space), outs),
        scratch_shapes=list(scratch),
        compiler_params=pltpu.CompilerParams(vmem_limit_bytes=room * 1024 * 1024),
        cost_estimate=pl.CostEstimate(flops=0, bytes_accessed=size, transcendentals=0),
    )(*operands)


def dot(left, right, left_dim, right_dim):
    return lax.dot_general(
        left, right, (((left_dim,), (right_dim,)), ((), ())), preferred_element_type=F32
    )


def iota(shape, dim):
    return lax.broadcasted_iota(jnp.int32, shape, dim)


def packed(blocks, last):
    rows = last.shape[0]
    place = iota(last.shape, 0) & 7
    groups = [
        jnp.where(place >= CAP, pltpu.roll(last, CAP - 2 * j, 0), block).reshape(
            rows // 8, 8, LANES
        )
        for j, block in enumerate(blocks)
    ]
    return jnp.concatenate(groups, axis=1).astype(BF16)


def unpacked(message):
    wide = message.astype(F32)
    rows = wide.shape[0] * 8
    blocks = [wide[:, 8 * j : 8 * j + 8, :].reshape(rows, LANES) for j in range(3)]
    place = iota((rows, LANES), 0) & 7
    moved = [pltpu.roll(block, rows - CAP + 2 * j, 0) for j, block in enumerate(blocks)]
    last = jnp.where(place < 2, moved[0], jnp.where(place < 4, moved[1], moved[2]))
    last = jnp.where(iota((rows, LANES), 1) >= LANES // 2, last, 0.0)
    return [v.astype(BF16) for v in blocks + [last]]


def dispatch_kernel(routes, gates, grads_t, message, chooser):
    held = message.shape[0]
    tokens = routes.shape[1]
    ids = routes[...]
    experts = iota((held, tokens), 0)
    first, second = ids[0:1] == experts, ids[1:2] == experts
    named = jnp.where(first | second, 1.0, 0.0).astype(BF16)
    before = jnp.where(
        iota((tokens, tokens), 0) < iota((tokens, tokens), 1), 1.0, 0.0
    ).astype(BF16)
    place = experts * 8 + dot(named, before, 1, 0).astype(jnp.int32) + 1
    row = iota((held * 8, tokens), 0) + 1
    hit_first = jnp.sum(jnp.where(first, place, 0), axis=0, keepdims=True) == row
    hit_second = jnp.sum(jnp.where(second, place, 0), axis=0, keepdims=True) == row
    weight = gates[...]
    gate = jnp.sum(
        jnp.where(hit_first, weight[0:1], 0.0) + jnp.where(hit_second, weight[1:2], 0.0),
        axis=1,
        keepdims=True,
    )
    chosen = jnp.where(hit_first | hit_second, 1.0, 0.0).astype(BF16)
    chooser[...] = chosen
    width = grads_t.shape[0]
    rows = dot(chosen, grads_t[...], 1, 1)
    tail = dot(chosen, grads_t[width - LANES :, :], 1, 1) * gate
    message[...] = packed(
        [rows[:, LANES * j : LANES * (j + 1)] * gate for j in range(3)], tail
    )


def down_kernel(arrived, down_t, mid, held_out, sems):
    cores, held = arrived.shape[0], arrived.shape[1]
    blocks = unpacked(arrived[...].reshape(cores * held, 3 * 8, LANES))
    slots, rows = cores * held * CAP, cores * held * 8
    row = iota((slots, rows), 1)
    core = jnp.where(row >= held * 8, 1, 0)
    block = ((row - core * held * 8) >> 3) * 2 + core
    pick = ((row & 7) < CAP) & (block * CAP + (row & 7) == iota((slots, rows), 0))
    pick = jnp.where(pick, 1.0, 0.0).astype(BF16)
    picked = dot(pick, jnp.concatenate(blocks, axis=1), 1, 0).astype(BF16)
    width = down_t.shape[0]
    weights = jnp.concatenate([down_t[: 3 * LANES, :], down_t[width - LANES :, :]], axis=0)
    total = dot(weights, picked, 0, 1)
    piece = mid.shape[1]
    copies = []
    for part in range(mid.shape[0]):
        held_out[part] = total[piece * part : piece * (part + 1)].astype(BF16)
        copies.append(pltpu.make_async_copy(held_out.at[part], mid.at[part], sems.at[part]))
        copies[part].start()
    for copy in copies:
        copy.wait()


def gate_kernel(shares, act, copies, held_out, sems):
    total = shares[0].astype(F32)
    for part in range(1, shares.shape[0]):
        total = total + shares[part].astype(F32)
    value = act[...].astype(F32)
    held_out[...] = (total * (value / (1.0 + jnp.exp(-value)))).astype(BF16)
    sent = [
        pltpu.make_async_copy(held_out, copies.at[part], sems.at[part])
        for part in range(copies.shape[0])
    ]
    for copy in sent:
        copy.start()
    for copy in sent:
        copy.wait()


def hold_kernel(weights, held_in, sem):
    copy = pltpu.make_async_copy(weights, held_in, sem)
    copy.start()
    copy.wait()


def up_kernel(full, up, rows_t, stacked):
    piece = full.shape[1]
    for part in range(full.shape[0]):
        stacked[piece * part : piece * (part + 1), :] = full[part].astype(F32)
    rows_t[...] = dot(up[...], stacked[...].astype(BF16), 1, 0).astype(BF16)


def return_kernel(core_id, halves, message):
    held = message.shape[0]
    slots = halves.shape[2]
    core = core_id[0]
    both = (halves[0].astype(F32) + halves[1].astype(F32)).astype(BF16)
    row = iota((held * 8, slots), 0)
    slot = ((row >> 3) * 2 + core) * CAP + (row & 7)
    pick = ((row & 7) < CAP) & (slot == iota((held * 8, slots), 1))
    pick = jnp.where(pick, 1.0, 0.0).astype(BF16)
    width = both.shape[0]
    rows = dot(pick, both, 1, 1)
    message[...] = packed(
        [rows[:, LANES * j : LANES * (j + 1)] for j in range(3)],
        dot(pick, both[width - LANES :], 1, 1),
    )


def combine_kernel(returned, chooser, dense_t, out_t):
    blocks = unpacked(returned[...])
    chosen = chooser[...]
    width = out_t.shape[0]
    for j in range(3):
        low = LANES * j
        out_t[low : low + LANES, :] = (
            dense_t[low : low + LANES, :] + dot(blocks[j], chosen, 0, 0)
        ).astype(BF16)
    half = LANES // 2
    out_t[3 * LANES :, :] = (
        dense_t[3 * LANES :, :] + dot(blocks[3], chosen, 0, 0)[half:]
    ).astype(BF16)


def wrapped(value, size):
    value = jnp.where(value >= size, value - size, value)
    return jnp.where(value < 0, value + size, value)


def dense_down_kernel(place, down_t, grads_t, *rest):
    slabs, blocks = rest[:-1], rest[-1]
    size = len(slabs)
    blocks[...] = dot(down_t[...], grads_t[...], 0, 0).reshape(blocks.shape)
    for step in range(size):
        first = wrapped(place[0] + step, size) * place[2]
        for second in range(size):
            slabs[step][second] = blocks[first + second * place[3]].astype(BF16)


def dense_sum_kernel(place, *rest):
    size = len(rest) // 2
    slabs, sums = rest[:size], rest[size:]
    for step in range(size):
        second = wrapped(place[1] + step, size)
        total = slabs[0][second].astype(F32)
        for slab in slabs[1:]:
            total = total + slab[second].astype(F32)
        sums[step][...] = total.astype(sums[step].dtype)


def dense_gate_kernel(*rest):
    pieces, act, hidden = rest[:-2], rest[-2], rest[-1]
    total = pieces[0][...].astype(F32)
    for piece in pieces[1:]:
        total = total + piece[...].astype(F32)
    value = act[...].astype(F32)
    hidden[...] = (total * (value / (1.0 + jnp.exp(-value)))).astype(BF16)


def dense_up_kernel(place, *rest):
    slabs, up, out_t, blocks = rest[:-3], rest[-3], rest[-2], rest[-1]
    size = len(slabs)
    for back in range(size):
        first = wrapped(place[0] - back, size) * place[2]
        for step in range(size):
            second = wrapped(place[1] - step, size) * place[3]
            blocks[first + second] = slabs[back][step].astype(F32)
    full = blocks[...].reshape(up.shape[1], blocks.shape[2]).astype(BF16)
    out_t[...] = dot(up[...], full, 1, 0)


def moved(value, stage, step, size):
    pairs = []
    for core in range(2):
        for x in range(size):
            for y in range(size):
                if core == stage:
                    target = ((x + step) % size, y)
                else:
                    target = (x, (y + step) % size)
                pairs.append(
                    ((core * size + x) * size + y, (core * size + target[0]) * size + target[1])
                )
    return lax.ppermute(value, ("c", "x", "y"), pairs)


def shards(
    grads, routes, gates, dense_down, dense_up, dense_act, expert_down, expert_up, expert_act
):
    held = lax.axis_size("z")
    across, along = lax.axis_size("x"), lax.axis_size("y")
    parts = across * along
    tokens, width = grads.shape
    half = expert_down.shape[1]
    piece, share = half // parts, dense_act.shape[1]
    slots = expert_act.shape[1]
    tensor = ("x", "y")

    message, chooser = call(
        dispatch_kernel,
        (
            jax.ShapeDtypeStruct((held, 24, LANES), BF16),
            jax.ShapeDtypeStruct((held * 8, tokens), BF16),
        ),
        routes.T,
        gates.T,
        grads.T,
        room=ROOM,
    )
    core, x, y = lax.axis_index("c"), lax.axis_index("x"), lax.axis_index("y")
    place = jnp.stack(
        [
            jnp.where(core == 0, x, y),
            jnp.where(core == 0, y, x),
            jnp.where(core == 0, along, 1),
            jnp.where(core == 0, 1, along),
        ]
    ).astype(jnp.int32)
    smem, vmem = pltpu.SMEM, pltpu.VMEM
    slab = jax.ShapeDtypeStruct((along, share, tokens), BF16)
    piece_f32 = jax.ShapeDtypeStruct((share, tokens), F32)
    piece_bf16 = jax.ShapeDtypeStruct((share, tokens), BF16)
    blocks = pltpu.VMEM((parts, share, tokens), F32)
    steps = range(1, along)

    message, dense_rows = lax.optimization_barrier((message, grads.T))
    arrived = lax.all_to_all(message, "z", 0, 0, tiled=True)
    slabs = call(
        dense_down_kernel,
        (slab,) * along,
        place,
        dense_down.T,
        dense_rows,
        scratch=[blocks],
        spaces=[smem, vmem, vmem],
    )
    sums = call(
        dense_sum_kernel,
        (piece_f32,) + (piece_bf16,) * (along - 1),
        place,
        slabs[0],
        *[moved(slabs[step], 0, step, along) for step in steps],
        spaces=[smem] + [vmem] * along,
    )
    arrived, sums = lax.optimization_barrier((arrived, sums))

    parts_out = jax.ShapeDtypeStruct((parts, piece, slots), BF16)
    mid = call(
        down_kernel,
        parts_out,
        lax.all_gather(arrived, "c", axis=0, tiled=False),
        expert_down[0].T,
        scratch=[pltpu.VMEM((parts, piece, slots), BF16), pltpu.SemaphoreType.DMA((parts,))],
        out_space=pltpu.HBM,
    )
    mid, sums, up = lax.optimization_barrier((mid, sums, expert_up[0]))
    shares = lax.all_to_all(mid, tensor, 0, 0, tiled=True)
    up = call(
        hold_kernel,
        jax.ShapeDtypeStruct((width, half), BF16),
        up,
        scratch=[pltpu.SemaphoreType.DMA],
        spaces=[pltpu.HBM],
        room=2,
    )
    pieces = [sums[0]] + [moved(sums[step], 1, step, along) for step in steps]
    shares, pieces, up = lax.optimization_barrier((shares, pieces, up))
    copies = call(
        gate_kernel,
        parts_out,
        shares,
        expert_act[0].T,
        scratch=[pltpu.VMEM((piece, slots), BF16), pltpu.SemaphoreType.DMA((parts,))],
        out_space=pltpu.HBM,
    )
    copies, pieces = lax.optimization_barrier((copies, pieces))
    full = lax.all_to_all(copies, tensor, 0, 0, tiled=True)
    full, pieces = lax.optimization_barrier((full, pieces))
    rows_t = call(
        up_kernel,
        jax.ShapeDtypeStruct((width, slots), BF16),
        full,
        up,
        scratch=[pltpu.VMEM((half, slots), F32)],
    )
    back = call(
        return_kernel,
        jax.ShapeDtypeStruct((held, 24, LANES), BF16),
        core.astype(jnp.int32).reshape(1),
        lax.all_gather(rows_t, "c", axis=0, tiled=False),
        spaces=[smem, vmem],
    )
    back, pieces = lax.optimization_barrier((back, pieces))
    returned = lax.all_to_all(back, "z", 0, 0, tiled=True)
    hidden = call(dense_gate_kernel, piece_bf16, *pieces, dense_act.T)
    columns = [hidden] + [moved(hidden, 1, step, along) for step in steps]
    column = jnp.stack(columns)
    dense_t = call(
        dense_up_kernel,
        jax.ShapeDtypeStruct((width, tokens), F32),
        place,
        column,
        *[moved(column, 0, step, along) for step in steps],
        dense_up,
        scratch=[blocks],
        spaces=[smem] + [vmem] * (along + 1),
    )
    out_t = call(
        combine_kernel, jax.ShapeDtypeStruct((width, tokens), BF16), returned, chooser, dense_t
    )
    return out_t.T


def solution(mesh):
    groups, parts = mesh.devices.shape
    across = 4 if parts == 16 else 2
    split = Mesh(
        mesh.devices.reshape(groups // 2, 2, across, parts // across), ("z", "c", "x", "y")
    )
    blocks, tensor = ("z", "c"), ("x", "y")
    placed = (
        P(blocks, tensor),
        P(blocks, None),
        P(blocks, None),
        P(None, tensor),
        P(tensor, None),
        P(blocks, tensor),
        P(blocks, None, tensor),
        P(blocks, tensor, None),
        P(blocks, None, tensor),
    )
    return jax.shard_map(
        shards, mesh=split, in_specs=placed, out_specs=P(blocks, tensor), check_vma=False
    )
```

```python
import jax
import jax.numpy as jnp
from jax import lax
from jax.experimental import pallas as pl
from jax.experimental.pallas import tpu as pltpu
from jax.sharding import Mesh, PartitionSpec as P

CAP = 6
LANES = 128
ROOM = 60
F32 = jnp.float32
BF16 = jnp.bfloat16


def call(kernel, outs, *operands, room=20, scratch=(), spaces=None, out_space=pltpu.VMEM):
    size = sum(v.size * v.dtype.itemsize for v in operands)
    spaces = spaces or [pltpu.VMEM] * len(operands)
    return pl.pallas_call(
        kernel,
        out_shape=outs,
        in_specs=[pl.BlockSpec(memory_space=space) for space in spaces],
        out_specs=jax.tree.map(lambda _: pl.BlockSpec(memory_space=out_space), outs),
        scratch_shapes=list(scratch),
        compiler_params=pltpu.CompilerParams(vmem_limit_bytes=room * 1024 * 1024),
        cost_estimate=pl.CostEstimate(flops=0, bytes_accessed=size, transcendentals=0),
    )(*operands)


def dot(left, right, left_dim, right_dim):
    return lax.dot_general(
        left, right, (((left_dim,), (right_dim,)), ((), ())), preferred_element_type=F32
    )


def iota(shape, dim):
    return lax.broadcasted_iota(jnp.int32, shape, dim)


def packed(blocks, last):
    rows = last.shape[0]
    place = iota(last.shape, 0) & 7
    groups = [
        jnp.where(place >= CAP, pltpu.roll(last, CAP - 2 * j, 0), block).reshape(
            rows // 8, 8, LANES
        )
        for j, block in enumerate(blocks)
    ]
    return jnp.concatenate(groups, axis=1).astype(BF16)


def unpacked(message):
    wide = message.astype(F32)
    rows = wide.shape[0] * 8
    blocks = [wide[:, 8 * j : 8 * j + 8, :].reshape(rows, LANES) for j in range(3)]
    place = iota((rows, LANES), 0) & 7
    moved = [pltpu.roll(block, rows - CAP + 2 * j, 0) for j, block in enumerate(blocks)]
    last = jnp.where(place < 2, moved[0], jnp.where(place < 4, moved[1], moved[2]))
    last = jnp.where(iota((rows, LANES), 1) >= LANES // 2, last, 0.0)
    return [v.astype(BF16) for v in blocks + [last]]


def dispatch_kernel(routes, gates, grads_t, message, chooser):
    held = message.shape[0]
    tokens = routes.shape[1]
    ids = routes[...]
    experts = iota((held, tokens), 0)
    first, second = ids[0:1] == experts, ids[1:2] == experts
    named = jnp.where(first | second, 1.0, 0.0).astype(BF16)
    before = jnp.where(
        iota((tokens, tokens), 0) < iota((tokens, tokens), 1), 1.0, 0.0
    ).astype(BF16)
    place = experts * 8 + dot(named, before, 1, 0).astype(jnp.int32) + 1
    row = iota((held * 8, tokens), 0) + 1
    hit_first = jnp.sum(jnp.where(first, place, 0), axis=0, keepdims=True) == row
    hit_second = jnp.sum(jnp.where(second, place, 0), axis=0, keepdims=True) == row
    weight = gates[...]
    gate = jnp.sum(
        jnp.where(hit_first, weight[0:1], 0.0) + jnp.where(hit_second, weight[1:2], 0.0),
        axis=1,
        keepdims=True,
    )
    chosen = jnp.where(hit_first | hit_second, 1.0, 0.0).astype(BF16)
    chooser[...] = chosen
    width = grads_t.shape[0]
    rows = dot(chosen, grads_t[...], 1, 1)
    tail = dot(chosen, grads_t[width - LANES :, :], 1, 1) * gate
    message[...] = packed(
        [rows[:, LANES * j : LANES * (j + 1)] * gate for j in range(3)], tail
    )


def down_kernel(arrived, down_t, mid, held_out, sems):
    cores, held = arrived.shape[0], arrived.shape[1]
    blocks = unpacked(arrived[...].reshape(cores * held, 3 * 8, LANES))
    slots, rows = cores * held * CAP, cores * held * 8
    row = iota((slots, rows), 1)
    core = jnp.where(row >= held * 8, 1, 0)
    block = ((row - core * held * 8) >> 3) * 2 + core
    pick = ((row & 7) < CAP) & (block * CAP + (row & 7) == iota((slots, rows), 0))
    pick = jnp.where(pick, 1.0, 0.0).astype(BF16)
    picked = dot(pick, jnp.concatenate(blocks, axis=1), 1, 0).astype(BF16)
    width = down_t.shape[0]
    weights = jnp.concatenate([down_t[: 3 * LANES, :], down_t[width - LANES :, :]], axis=0)
    total = dot(weights, picked, 0, 1)
    piece = mid.shape[1]
    copies = []
    for part in range(mid.shape[0]):
        held_out[part] = total[piece * part : piece * (part + 1)].astype(BF16)
        copies.append(pltpu.make_async_copy(held_out.at[part], mid.at[part], sems.at[part]))
        copies[part].start()
    for copy in copies:
        copy.wait()


def gate_kernel(shares, act, copies, held_out, sems):
    total = shares[0].astype(F32)
    for part in range(1, shares.shape[0]):
        total = total + shares[part].astype(F32)
    value = act[...].astype(F32)
    held_out[...] = (total * (value / (1.0 + jnp.exp(-value)))).astype(BF16)
    sent = [
        pltpu.make_async_copy(held_out, copies.at[part], sems.at[part])
        for part in range(copies.shape[0])
    ]
    for copy in sent:
        copy.start()
    for copy in sent:
        copy.wait()


def hold_kernel(weights, held_in, sem):
    copy = pltpu.make_async_copy(weights, held_in, sem)
    copy.start()
    copy.wait()


def up_kernel(full, up, rows_t, stacked):
    piece = full.shape[1]
    for part in range(full.shape[0]):
        stacked[piece * part : piece * (part + 1), :] = full[part].astype(F32)
    rows_t[...] = dot(up[...], stacked[...].astype(BF16), 1, 0).astype(BF16)


def return_kernel(core_id, halves, message):
    held = message.shape[0]
    slots = halves.shape[2]
    core = core_id[0]
    both = (halves[0].astype(F32) + halves[1].astype(F32)).astype(BF16)
    row = iota((held * 8, slots), 0)
    slot = ((row >> 3) * 2 + core) * CAP + (row & 7)
    pick = ((row & 7) < CAP) & (slot == iota((held * 8, slots), 1))
    pick = jnp.where(pick, 1.0, 0.0).astype(BF16)
    width = both.shape[0]
    rows = dot(pick, both, 1, 1)
    message[...] = packed(
        [rows[:, LANES * j : LANES * (j + 1)] for j in range(3)],
        dot(pick, both[width - LANES :], 1, 1),
    )


def combine_kernel(returned, chooser, dense_t, out_t):
    blocks = unpacked(returned[...])
    chosen = chooser[...]
    width = out_t.shape[0]
    for j in range(3):
        low = LANES * j
        out_t[low : low + LANES, :] = (
            dense_t[low : low + LANES, :] + dot(blocks[j], chosen, 0, 0)
        ).astype(BF16)
    half = LANES // 2
    out_t[3 * LANES :, :] = (
        dense_t[3 * LANES :, :] + dot(blocks[3], chosen, 0, 0)[half:]
    ).astype(BF16)


def wrapped(value, size):
    value = jnp.where(value >= size, value - size, value)
    return jnp.where(value < 0, value + size, value)


def dense_down_kernel(place, down_t, grads_t, *rest):
    slabs, blocks = rest[:-1], rest[-1]
    size = len(slabs)
    blocks[...] = dot(down_t[...], grads_t[...], 0, 0).reshape(blocks.shape)
    for step in range(size):
        first = wrapped(place[0] + step, size) * place[2]
        for second in range(size):
            slabs[step][second] = blocks[first + second * place[3]].astype(BF16)


def dense_sum_kernel(place, *rest):
    size = len(rest) // 2
    slabs, sums = rest[:size], rest[size:]
    for step in range(size):
        second = wrapped(place[1] + step, size)
        total = slabs[0][second].astype(F32)
        for slab in slabs[1:]:
            total = total + slab[second].astype(F32)
        sums[step][...] = total.astype(sums[step].dtype)


def dense_gate_kernel(*rest):
    pieces, act, hidden = rest[:-2], rest[-2], rest[-1]
    total = pieces[0][...].astype(F32)
    for piece in pieces[1:]:
        total = total + piece[...].astype(F32)
    value = act[...].astype(F32)
    hidden[...] = (total * (value / (1.0 + jnp.exp(-value)))).astype(BF16)


def dense_up_kernel(place, *rest):
    slabs, up, out_t, blocks = rest[:-3], rest[-3], rest[-2], rest[-1]
    size = len(slabs)
    for back in range(size):
        first = wrapped(place[0] - back, size) * place[2]
        for step in range(size):
            second = wrapped(place[1] - step, size) * place[3]
            blocks[first + second] = slabs[back][step].astype(F32)
    full = blocks[...].reshape(up.shape[1], blocks.shape[2]).astype(BF16)
    out_t[...] = dot(up[...], full, 1, 0)


def moved(value, stage, step, size):
    pairs = []
    for core in range(2):
        for x in range(size):
            for y in range(size):
                if core == stage:
                    target = ((x + step) % size, y)
                else:
                    target = (x, (y + step) % size)
                pairs.append(
                    ((core * size + x) * size + y, (core * size + target[0]) * size + target[1])
                )
    return lax.ppermute(value, ("c", "x", "y"), pairs)


def shards(
    grads, routes, gates, dense_down, dense_up, dense_act, expert_down, expert_up, expert_act
):
    held = lax.axis_size("z")
    across, along = lax.axis_size("x"), lax.axis_size("y")
    parts = across * along
    tokens, width = grads.shape
    half = expert_down.shape[1]
    piece, share = half // parts, dense_act.shape[1]
    slots = expert_act.shape[1]
    tensor = ("x", "y")

    message, chooser = call(
        dispatch_kernel,
        (
            jax.ShapeDtypeStruct((held, 24, LANES), BF16),
            jax.ShapeDtypeStruct((held * 8, tokens), BF16),
        ),
        routes.T,
        gates.T,
        grads.T,
        room=ROOM,
    )
    core, x, y = lax.axis_index("c"), lax.axis_index("x"), lax.axis_index("y")
    place = jnp.stack(
        [
            jnp.where(core == 0, x, y),
            jnp.where(core == 0, y, x),
            jnp.where(core == 0, along, 1),
            jnp.where(core == 0, 1, along),
        ]
    ).astype(jnp.int32)
    smem, vmem = pltpu.SMEM, pltpu.VMEM
    slab = jax.ShapeDtypeStruct((along, share, tokens), BF16)
    piece_f32 = jax.ShapeDtypeStruct((share, tokens), F32)
    piece_bf16 = jax.ShapeDtypeStruct((share, tokens), BF16)
    blocks = pltpu.VMEM((parts, share, tokens), F32)
    steps = range(1, along)

    message, dense_rows = lax.optimization_barrier((message, grads.T))
    arrived = lax.all_to_all(message, "z", 0, 0, tiled=True)
    slabs = call(
        dense_down_kernel,
        (slab,) * along,
        place,
        dense_down.T,
        dense_rows,
        scratch=[blocks],
        spaces=[smem, vmem, vmem],
    )
    sums = call(
        dense_sum_kernel,
        (piece_f32,) + (piece_bf16,) * (along - 1),
        place,
        slabs[0],
        *[moved(slabs[step], 0, step, along) for step in steps],
        spaces=[smem] + [vmem] * along,
    )
    arrived, sums = lax.optimization_barrier((arrived, sums))

    parts_out = jax.ShapeDtypeStruct((parts, piece, slots), BF16)
    mid = call(
        down_kernel,
        parts_out,
        lax.all_gather(arrived, "c", axis=0, tiled=False),
        expert_down[0].T,
        scratch=[pltpu.VMEM((parts, piece, slots), BF16), pltpu.SemaphoreType.DMA((parts,))],
        out_space=pltpu.HBM,
    )
    mid, sums = lax.optimization_barrier((mid, sums))
    shares = lax.all_to_all(mid, tensor, 0, 0, tiled=True)
    pieces = [sums[0]] + [moved(sums[step], 1, step, along) for step in steps]
    shares, pieces = lax.optimization_barrier((shares, pieces))
    copies = call(
        gate_kernel,
        parts_out,
        shares,
        expert_act[0].T,
        scratch=[pltpu.VMEM((piece, slots), BF16), pltpu.SemaphoreType.DMA((parts,))],
        out_space=pltpu.HBM,
    )
    copies, pieces, up = lax.optimization_barrier((copies, pieces, expert_up[0]))
    full = lax.all_to_all(copies, tensor, 0, 0, tiled=True)
    up = call(
        hold_kernel,
        jax.ShapeDtypeStruct((width, half), BF16),
        up,
        scratch=[pltpu.SemaphoreType.DMA],
        spaces=[pltpu.HBM],
        room=2,
    )
    full, pieces, up = lax.optimization_barrier((full, pieces, up))
    rows_t = call(
        up_kernel,
        jax.ShapeDtypeStruct((width, slots), BF16),
        full,
        up,
        scratch=[pltpu.VMEM((half, slots), F32)],
    )
    back = call(
        return_kernel,
        jax.ShapeDtypeStruct((held, 24, LANES), BF16),
        core.astype(jnp.int32).reshape(1),
        lax.all_gather(rows_t, "c", axis=0, tiled=False),
        spaces=[smem, vmem],
    )
    back, pieces = lax.optimization_barrier((back, pieces))
    returned = lax.all_to_all(back, "z", 0, 0, tiled=True)
    hidden = call(dense_gate_kernel, piece_bf16, *pieces, dense_act.T)
    columns = [hidden] + [moved(hidden, 1, step, along) for step in steps]
    column = jnp.stack(columns)
    dense_t = call(
        dense_up_kernel,
        jax.ShapeDtypeStruct((width, tokens), F32),
        place,
        column,
        *[moved(column, 0, step, along) for step in steps],
        dense_up,
        scratch=[blocks],
        spaces=[smem] + [vmem] * (along + 1),
    )
    out_t = call(
        combine_kernel, jax.ShapeDtypeStruct((width, tokens), BF16), returned, chooser, dense_t
    )
    return out_t.T


def solution(mesh):
    groups, parts = mesh.devices.shape
    across = 4 if parts == 16 else 2
    split = Mesh(
        mesh.devices.reshape(groups // 2, 2, across, parts // across), ("z", "c", "x", "y")
    )
    blocks, tensor = ("z", "c"), ("x", "y")
    placed = (
        P(blocks, tensor),
        P(blocks, None),
        P(blocks, None),
        P(None, tensor),
        P(tensor, None),
        P(blocks, tensor),
        P(blocks, None, tensor),
        P(blocks, tensor, None),
        P(blocks, None, tensor),
    )
    return jax.shard_map(
        shards, mesh=split, in_specs=placed, out_specs=P(blocks, tensor), check_vma=False
    )
```

```python
import jax
import jax.numpy as jnp
from jax import lax
from jax.experimental import pallas as pl
from jax.experimental.pallas import tpu as pltpu
from jax.sharding import Mesh, PartitionSpec as P

CAP = 6
LANES = 128
ROOM = 60
F32 = jnp.float32
BF16 = jnp.bfloat16


def call(kernel, outs, *operands, room=20, scratch=(), spaces=None, out_space=pltpu.VMEM):
    size = sum(v.size * v.dtype.itemsize for v in operands)
    spaces = spaces or [pltpu.VMEM] * len(operands)
    return pl.pallas_call(
        kernel,
        out_shape=outs,
        in_specs=[pl.BlockSpec(memory_space=space) for space in spaces],
        out_specs=jax.tree.map(lambda _: pl.BlockSpec(memory_space=out_space), outs),
        scratch_shapes=list(scratch),
        compiler_params=pltpu.CompilerParams(vmem_limit_bytes=room * 1024 * 1024),
        cost_estimate=pl.CostEstimate(flops=0, bytes_accessed=size, transcendentals=0),
    )(*operands)


def dot(left, right, left_dim, right_dim):
    return lax.dot_general(
        left, right, (((left_dim,), (right_dim,)), ((), ())), preferred_element_type=F32
    )


def iota(shape, dim):
    return lax.broadcasted_iota(jnp.int32, shape, dim)


def packed(blocks, last):
    rows = last.shape[0]
    place = iota(last.shape, 0) & 7
    groups = [
        jnp.where(place >= CAP, pltpu.roll(last, CAP - 2 * j, 0), block).reshape(
            rows // 8, 8, LANES
        )
        for j, block in enumerate(blocks)
    ]
    return jnp.concatenate(groups, axis=1).astype(BF16)


def unpacked(message):
    wide = message.astype(F32)
    rows = wide.shape[0] * 8
    blocks = [wide[:, 8 * j : 8 * j + 8, :].reshape(rows, LANES) for j in range(3)]
    place = iota((rows, LANES), 0) & 7
    moved = [pltpu.roll(block, rows - CAP + 2 * j, 0) for j, block in enumerate(blocks)]
    last = jnp.where(place < 2, moved[0], jnp.where(place < 4, moved[1], moved[2]))
    last = jnp.where(iota((rows, LANES), 1) >= LANES // 2, last, 0.0)
    return [v.astype(BF16) for v in blocks + [last]]


def dispatch_kernel(routes, gates, grads_t, message, chooser):
    held = message.shape[0]
    tokens = routes.shape[1]
    ids = routes[...]
    experts = iota((held, tokens), 0)
    first, second = ids[0:1] == experts, ids[1:2] == experts
    named = jnp.where(first | second, 1.0, 0.0).astype(BF16)
    before = jnp.where(
        iota((tokens, tokens), 0) < iota((tokens, tokens), 1), 1.0, 0.0
    ).astype(BF16)
    place = experts * 8 + dot(named, before, 1, 0).astype(jnp.int32) + 1
    row = iota((held * 8, tokens), 0) + 1
    hit_first = jnp.sum(jnp.where(first, place, 0), axis=0, keepdims=True) == row
    hit_second = jnp.sum(jnp.where(second, place, 0), axis=0, keepdims=True) == row
    weight = gates[...]
    gate = jnp.sum(
        jnp.where(hit_first, weight[0:1], 0.0) + jnp.where(hit_second, weight[1:2], 0.0),
        axis=1,
        keepdims=True,
    )
    chosen = jnp.where(hit_first | hit_second, 1.0, 0.0).astype(BF16)
    chooser[...] = chosen
    width = grads_t.shape[0]
    rows = dot(chosen, grads_t[...], 1, 1)
    tail = dot(chosen, grads_t[width - LANES :, :], 1, 1) * gate
    message[...] = packed(
        [rows[:, LANES * j : LANES * (j + 1)] * gate for j in range(3)], tail
    )


def down_kernel(arrived, down_t, mid, held_out, sems):
    cores, held = arrived.shape[0], arrived.shape[1]
    blocks = unpacked(arrived[...].reshape(cores * held, 3 * 8, LANES))
    slots, rows = cores * held * CAP, cores * held * 8
    row = iota((slots, rows), 1)
    core = jnp.where(row >= held * 8, 1, 0)
    block = ((row - core * held * 8) >> 3) * 2 + core
    pick = ((row & 7) < CAP) & (block * CAP + (row & 7) == iota((slots, rows), 0))
    pick = jnp.where(pick, 1.0, 0.0).astype(BF16)
    picked = dot(pick, jnp.concatenate(blocks, axis=1), 1, 0).astype(BF16)
    width = down_t.shape[0]
    weights = jnp.concatenate([down_t[: 3 * LANES, :], down_t[width - LANES :, :]], axis=0)
    total = dot(weights, picked, 0, 1)
    piece = mid.shape[1]
    copies = []
    for part in range(mid.shape[0]):
        held_out[part] = total[piece * part : piece * (part + 1)].astype(BF16)
        copies.append(pltpu.make_async_copy(held_out.at[part], mid.at[part], sems.at[part]))
        copies[part].start()
    for copy in copies:
        copy.wait()


def gate_kernel(shares, act, copies, held_out, sems):
    total = shares[0].astype(F32)
    for part in range(1, shares.shape[0]):
        total = total + shares[part].astype(F32)
    value = act[...].astype(F32)
    held_out[...] = (total * (value / (1.0 + jnp.exp(-value)))).astype(BF16)
    sent = [
        pltpu.make_async_copy(held_out, copies.at[part], sems.at[part])
        for part in range(copies.shape[0])
    ]
    for copy in sent:
        copy.start()
    for copy in sent:
        copy.wait()


def hold_kernel(weights, held_in, sem):
    copy = pltpu.make_async_copy(weights, held_in, sem)
    copy.start()
    copy.wait()


def up_kernel(full, up, rows_t, stacked):
    piece = full.shape[1]
    for part in range(full.shape[0]):
        stacked[piece * part : piece * (part + 1), :] = full[part].astype(F32)
    rows_t[...] = dot(up[...], stacked[...].astype(BF16), 1, 0).astype(BF16)


def return_kernel(core_id, halves, message):
    held = message.shape[0]
    slots = halves.shape[2]
    core = core_id[0]
    both = (halves[0].astype(F32) + halves[1].astype(F32)).astype(BF16)
    row = iota((held * 8, slots), 0)
    slot = ((row >> 3) * 2 + core) * CAP + (row & 7)
    pick = ((row & 7) < CAP) & (slot == iota((held * 8, slots), 1))
    pick = jnp.where(pick, 1.0, 0.0).astype(BF16)
    width = both.shape[0]
    rows = dot(pick, both, 1, 1)
    message[...] = packed(
        [rows[:, LANES * j : LANES * (j + 1)] for j in range(3)],
        dot(pick, both[width - LANES :], 1, 1),
    )


def combine_kernel(returned, chooser, dense_t, out_t):
    blocks = unpacked(returned[...])
    chosen = chooser[...]
    width = out_t.shape[0]
    for j in range(3):
        low = LANES * j
        out_t[low : low + LANES, :] = (
            dense_t[low : low + LANES, :] + dot(blocks[j], chosen, 0, 0)
        ).astype(BF16)
    half = LANES // 2
    out_t[3 * LANES :, :] = (
        dense_t[3 * LANES :, :] + dot(blocks[3], chosen, 0, 0)[half:]
    ).astype(BF16)


def wrapped(value, size):
    value = jnp.where(value >= size, value - size, value)
    return jnp.where(value < 0, value + size, value)


def dense_down_kernel(place, down_t, grads_t, *rest):
    slabs, blocks = rest[:-1], rest[-1]
    size = len(slabs)
    blocks[...] = dot(down_t[...], grads_t[...], 0, 0).reshape(blocks.shape)
    for step in range(size):
        first = wrapped(place[0] + step, size) * place[2]
        for second in range(size):
            slabs[step][second] = blocks[first + second * place[3]].astype(BF16)


def dense_sum_kernel(place, *rest):
    size = len(rest) // 2
    slabs, sums = rest[:size], rest[size:]
    for step in range(size):
        second = wrapped(place[1] + step, size)
        total = slabs[0][second].astype(F32)
        for slab in slabs[1:]:
            total = total + slab[second].astype(F32)
        sums[step][...] = total.astype(sums[step].dtype)


def dense_gate_kernel(*rest):
    pieces, act, hidden = rest[:-2], rest[-2], rest[-1]
    total = pieces[0][...].astype(F32)
    for piece in pieces[1:]:
        total = total + piece[...].astype(F32)
    value = act[...].astype(F32)
    hidden[...] = (total * (value / (1.0 + jnp.exp(-value)))).astype(BF16)


def dense_up_kernel(place, *rest):
    slabs, up, out_t, blocks = rest[:-3], rest[-3], rest[-2], rest[-1]
    size = len(slabs)
    for back in range(size):
        first = wrapped(place[0] - back, size) * place[2]
        for step in range(size):
            second = wrapped(place[1] - step, size) * place[3]
            blocks[first + second] = slabs[back][step].astype(F32)
    full = blocks[...].reshape(up.shape[1], blocks.shape[2]).astype(BF16)
    out_t[...] = dot(up[...], full, 1, 0)


def moved(value, stage, step, size):
    pairs = []
    for core in range(2):
        for x in range(size):
            for y in range(size):
                if core == stage:
                    target = ((x + step) % size, y)
                else:
                    target = (x, (y + step) % size)
                pairs.append(
                    ((core * size + x) * size + y, (core * size + target[0]) * size + target[1])
                )
    return lax.ppermute(value, ("c", "x", "y"), pairs)


def shards(
    grads, routes, gates, dense_down, dense_up, dense_act, expert_down, expert_up, expert_act
):
    held = lax.axis_size("z")
    across, along = lax.axis_size("x"), lax.axis_size("y")
    parts = across * along
    tokens, width = grads.shape
    half = expert_down.shape[1]
    piece, share = half // parts, dense_act.shape[1]
    slots = expert_act.shape[1]
    tensor = ("x", "y")

    message, chooser = call(
        dispatch_kernel,
        (
            jax.ShapeDtypeStruct((held, 24, LANES), BF16),
            jax.ShapeDtypeStruct((held * 8, tokens), BF16),
        ),
        routes.T,
        gates.T,
        grads.T,
        room=ROOM,
    )
    core, x, y = lax.axis_index("c"), lax.axis_index("x"), lax.axis_index("y")
    place = jnp.stack(
        [
            jnp.where(core == 0, x, y),
            jnp.where(core == 0, y, x),
            jnp.where(core == 0, along, 1),
            jnp.where(core == 0, 1, along),
        ]
    ).astype(jnp.int32)
    smem, vmem = pltpu.SMEM, pltpu.VMEM
    slab = jax.ShapeDtypeStruct((along, share, tokens), BF16)
    piece_f32 = jax.ShapeDtypeStruct((share, tokens), F32)
    piece_bf16 = jax.ShapeDtypeStruct((share, tokens), BF16)
    blocks = pltpu.VMEM((parts, share, tokens), F32)
    steps = range(1, along)

    message, dense_rows = lax.optimization_barrier((message, grads.T))
    arrived = lax.all_to_all(message, "z", 0, 0, tiled=True)
    slabs = call(
        dense_down_kernel,
        (slab,) * along,
        place,
        dense_down.T,
        dense_rows,
        scratch=[blocks],
        spaces=[smem, vmem, vmem],
    )
    slabs = [slabs[0]] + [moved(slabs[step], 0, step, along) for step in steps]
    arrived = lax.all_gather(arrived, "c", axis=0, tiled=False)
    arrived, slabs = lax.optimization_barrier((arrived, slabs))

    parts_out = jax.ShapeDtypeStruct((parts, piece, slots), BF16)
    mid = call(
        down_kernel,
        parts_out,
        arrived,
        expert_down[0].T,
        scratch=[pltpu.VMEM((parts, piece, slots), BF16), pltpu.SemaphoreType.DMA((parts,))],
        out_space=pltpu.HBM,
    )
    mid, slabs = lax.optimization_barrier((mid, slabs))
    shares = lax.all_to_all(mid, tensor, 0, 0, tiled=True)
    sums = call(
        dense_sum_kernel,
        (piece_f32,) + (piece_bf16,) * (along - 1),
        place,
        *slabs,
        spaces=[smem] + [vmem] * along,
    )
    pieces = [sums[0]] + [moved(sums[step], 1, step, along) for step in steps]
    shares, pieces = lax.optimization_barrier((shares, pieces))
    copies = call(
        gate_kernel,
        parts_out,
        shares,
        expert_act[0].T,
        scratch=[pltpu.VMEM((piece, slots), BF16), pltpu.SemaphoreType.DMA((parts,))],
        out_space=pltpu.HBM,
    )
    copies, pieces, up = lax.optimization_barrier((copies, pieces, expert_up[0]))
    full = lax.all_to_all(copies, tensor, 0, 0, tiled=True)
    up = call(
        hold_kernel,
        jax.ShapeDtypeStruct((width, half), BF16),
        up,
        scratch=[pltpu.SemaphoreType.DMA],
        spaces=[pltpu.HBM],
        room=2,
    )
    full, pieces, up = lax.optimization_barrier((full, pieces, up))
    rows_t = call(
        up_kernel,
        jax.ShapeDtypeStruct((width, slots), BF16),
        full,
        up,
        scratch=[pltpu.VMEM((half, slots), F32)],
    )
    back = call(
        return_kernel,
        jax.ShapeDtypeStruct((held, 24, LANES), BF16),
        core.astype(jnp.int32).reshape(1),
        lax.all_gather(rows_t, "c", axis=0, tiled=False),
        spaces=[smem, vmem],
    )
    back, pieces = lax.optimization_barrier((back, pieces))
    returned = lax.all_to_all(back, "z", 0, 0, tiled=True)
    hidden = call(dense_gate_kernel, piece_bf16, *pieces, dense_act.T)
    columns = [hidden] + [moved(hidden, 1, step, along) for step in steps]
    column = jnp.stack(columns)
    dense_t = call(
        dense_up_kernel,
        jax.ShapeDtypeStruct((width, tokens), F32),
        place,
        column,
        *[moved(column, 0, step, along) for step in steps],
        dense_up,
        scratch=[blocks],
        spaces=[smem] + [vmem] * (along + 1),
    )
    out_t = call(
        combine_kernel, jax.ShapeDtypeStruct((width, tokens), BF16), returned, chooser, dense_t
    )
    return out_t.T


def solution(mesh):
    groups, parts = mesh.devices.shape
    across = 4 if parts == 16 else 2
    split = Mesh(
        mesh.devices.reshape(groups // 2, 2, across, parts // across), ("z", "c", "x", "y")
    )
    blocks, tensor = ("z", "c"), ("x", "y")
    placed = (
        P(blocks, tensor),
        P(blocks, None),
        P(blocks, None),
        P(None, tensor),
        P(tensor, None),
        P(blocks, tensor),
        P(blocks, None, tensor),
        P(blocks, tensor, None),
        P(blocks, None, tensor),
    )
    return jax.shard_map(
        shards, mesh=split, in_specs=placed, out_specs=P(blocks, tensor), check_vma=False
    )
```

```python
import jax
import jax.numpy as jnp
from jax import lax
from jax.experimental import pallas as pl
from jax.experimental.pallas import tpu as pltpu
from jax.sharding import Mesh, PartitionSpec as P

CAP = 6
ROOM = 60
F32 = jnp.float32
BF16 = jnp.bfloat16


def call(kernel, outs, *operands, room=20, scratch=(), spaces=None, out_space=pltpu.VMEM):
    size = sum(v.size * v.dtype.itemsize for v in operands)
    spaces = spaces or [pltpu.VMEM] * len(operands)
    return pl.pallas_call(
        kernel,
        out_shape=outs,
        in_specs=[pl.BlockSpec(memory_space=space) for space in spaces],
        out_specs=jax.tree.map(lambda _: pl.BlockSpec(memory_space=out_space), outs),
        scratch_shapes=list(scratch),
        compiler_params=pltpu.CompilerParams(vmem_limit_bytes=room * 1024 * 1024),
        cost_estimate=pl.CostEstimate(flops=0, bytes_accessed=size, transcendentals=0),
    )(*operands)


def dot(left, right, left_dim, right_dim):
    return lax.dot_general(
        left, right, (((left_dim,), (right_dim,)), ((), ())), preferred_element_type=F32
    )


def iota(shape, dim):
    return lax.broadcasted_iota(jnp.int32, shape, dim)


def packed(rows):
    count = rows.shape[0] // CAP
    sides = [
        jnp.concatenate(
            [rows[count * (3 * side + i) : count * (3 * side + i + 1)] for i in range(3)], axis=1
        )
        for side in range(2)
    ]
    return jnp.stack(sides, axis=1).astype(BF16)


def unpacked(message):
    wide = message.astype(F32)
    width = wide.shape[2] // 3
    rows = [
        wide[:, side, width * i : width * (i + 1)] for side in range(2) for i in range(3)
    ]
    return jnp.concatenate(rows, axis=0).astype(BF16)


def dispatch_kernel(routes, gates, grads_t, message, chooser):
    held = message.shape[0]
    tokens = routes.shape[1]
    ids = routes[...]
    experts = iota((held, tokens), 0)
    first, second = ids[0:1] == experts, ids[1:2] == experts
    named = jnp.where(first | second, 1.0, 0.0).astype(BF16)
    before = jnp.where(
        iota((tokens, tokens), 0) < iota((tokens, tokens), 1), 1.0, 0.0
    ).astype(BF16)
    place = experts + dot(named, before, 1, 0).astype(jnp.int32) * held + 1
    row = iota((held * CAP, tokens), 0) + 1
    hit_first = jnp.sum(jnp.where(first, place, 0), axis=0, keepdims=True) == row
    hit_second = jnp.sum(jnp.where(second, place, 0), axis=0, keepdims=True) == row
    weight = gates[...]
    gate = jnp.sum(
        jnp.where(hit_first, weight[0:1], 0.0) + jnp.where(hit_second, weight[1:2], 0.0),
        axis=1,
        keepdims=True,
    )
    chosen = jnp.where(hit_first | hit_second, 1.0, 0.0).astype(BF16)
    chooser[...] = chosen
    message[...] = packed(dot(chosen, grads_t[...], 1, 1) * gate)


def down_kernel(arrived, down_t, mid, held_out, sems):
    cores, held = arrived.shape[0], arrived.shape[1]
    rows = unpacked(arrived[...].reshape((cores * held,) + arrived.shape[2:]))
    slots, sources = rows.shape[0], cores * held
    row = iota((slots, slots), 1)
    rank = row // sources
    source = row - rank * sources
    core = jnp.where(source >= held, 1, 0)
    slot = ((source - core * held) * 2 + core) * CAP + rank
    pick = jnp.where(slot == iota((slots, slots), 0), 1.0, 0.0).astype(BF16)
    picked = dot(pick, rows, 1, 0).astype(BF16)
    total = dot(down_t[...], picked, 0, 1)
    piece = mid.shape[1]
    copies = []
    for part in range(mid.shape[0]):
        held_out[part] = total[piece * part : piece * (part + 1)].astype(BF16)
        copies.append(pltpu.make_async_copy(held_out.at[part], mid.at[part], sems.at[part]))
        copies[part].start()
    for copy in copies:
        copy.wait()


def gate_kernel(shares, act, copies, held_out, sems):
    total = shares[0].astype(F32)
    for part in range(1, shares.shape[0]):
        total = total + shares[part].astype(F32)
    value = act[...].astype(F32)
    held_out[...] = (total * (value / (1.0 + jnp.exp(-value)))).astype(BF16)
    sent = [
        pltpu.make_async_copy(held_out, copies.at[part], sems.at[part])
        for part in range(copies.shape[0])
    ]
    for copy in sent:
        copy.start()
    for copy in sent:
        copy.wait()


def hold_kernel(weights, held_in, sem):
    copy = pltpu.make_async_copy(weights, held_in, sem)
    copy.start()
    copy.wait()


def up_kernel(full, up, rows_t, stacked):
    piece = full.shape[1]
    for part in range(full.shape[0]):
        stacked[piece * part : piece * (part + 1), :] = full[part].astype(F32)
    rows_t[...] = dot(up[...], stacked[...].astype(BF16), 1, 0).astype(BF16)


def return_kernel(core_id, halves, message):
    held = message.shape[0]
    slots = halves.shape[2]
    core = core_id[0]
    both = (halves[0].astype(F32) + halves[1].astype(F32)).astype(BF16)
    row = iota((held * CAP, slots), 0)
    rank = row // held
    slot = ((row - rank * held) * 2 + core) * CAP + rank
    pick = jnp.where(slot == iota((held * CAP, slots), 1), 1.0, 0.0).astype(BF16)
    message[...] = packed(dot(pick, both, 1, 1))


def combine_kernel(returned, chooser, dense_t, out_t):
    routed = dot(unpacked(returned[...]), chooser[...], 0, 0)
    out_t[...] = (dense_t[...] + routed).astype(BF16)


def wrapped(value, size):
    value = jnp.where(value >= size, value - size, value)
    return jnp.where(value < 0, value + size, value)


def dense_down_kernel(place, down_t, grads_t, *rest):
    slabs, blocks = rest[:-1], rest[-1]
    size = len(slabs)
    blocks[...] = dot(down_t[...], grads_t[...], 0, 0).reshape(blocks.shape)
    for step in range(size):
        first = wrapped(place[0] + step, size) * place[2]
        for second in range(size):
            slabs[step][second] = blocks[first + second * place[3]].astype(BF16)


def dense_sum_kernel(place, *rest):
    size = len(rest) // 2
    slabs, sums = rest[:size], rest[size:]
    for step in range(size):
        second = wrapped(place[1] + step, size)
        total = slabs[0][second].astype(F32)
        for slab in slabs[1:]:
            total = total + slab[second].astype(F32)
        sums[step][...] = total.astype(sums[step].dtype)


def dense_gate_kernel(*rest):
    pieces, act, hidden = rest[:-2], rest[-2], rest[-1]
    total = pieces[0][...].astype(F32)
    for piece in pieces[1:]:
        total = total + piece[...].astype(F32)
    value = act[...].astype(F32)
    hidden[...] = (total * (value / (1.0 + jnp.exp(-value)))).astype(BF16)


def dense_up_kernel(place, *rest):
    slabs, up, out_t, blocks = rest[:-3], rest[-3], rest[-2], rest[-1]
    size = len(slabs)
    for back in range(size):
        first = wrapped(place[0] - back, size) * place[2]
        for step in range(size):
            second = wrapped(place[1] - step, size) * place[3]
            blocks[first + second] = slabs[back][step].astype(F32)
    full = blocks[...].reshape(up.shape[1], blocks.shape[2]).astype(BF16)
    out_t[...] = dot(up[...], full, 1, 0)


def moved(value, stage, step, size):
    pairs = []
    for core in range(2):
        for x in range(size):
            for y in range(size):
                if core == stage:
                    target = ((x + step) % size, y)
                else:
                    target = (x, (y + step) % size)
                pairs.append(
                    ((core * size + x) * size + y, (core * size + target[0]) * size + target[1])
                )
    return lax.ppermute(value, ("c", "x", "y"), pairs)


def shards(
    grads, routes, gates, dense_down, dense_up, dense_act, expert_down, expert_up, expert_act
):
    held = lax.axis_size("z")
    across, along = lax.axis_size("x"), lax.axis_size("y")
    parts = across * along
    tokens, width = grads.shape
    half = expert_down.shape[1]
    piece, share = half // parts, dense_act.shape[1]
    slots = expert_act.shape[1]
    tensor = ("x", "y")

    message, chooser = call(
        dispatch_kernel,
        (
            jax.ShapeDtypeStruct((held, 2, 3 * width), BF16),
            jax.ShapeDtypeStruct((held * CAP, tokens), BF16),
        ),
        routes.T,
        gates.T,
        grads.T,
        room=ROOM,
    )
    core, x, y = lax.axis_index("c"), lax.axis_index("x"), lax.axis_index("y")
    place = jnp.stack(
        [
            jnp.where(core == 0, x, y),
            jnp.where(core == 0, y, x),
            jnp.where(core == 0, along, 1),
            jnp.where(core == 0, 1, along),
        ]
    ).astype(jnp.int32)
    smem, vmem = pltpu.SMEM, pltpu.VMEM
    slab = jax.ShapeDtypeStruct((along, share, tokens), BF16)
    piece_f32 = jax.ShapeDtypeStruct((share, tokens), F32)
    piece_bf16 = jax.ShapeDtypeStruct((share, tokens), BF16)
    blocks = pltpu.VMEM((parts, share, tokens), F32)
    steps = range(1, along)

    message, dense_rows = lax.optimization_barrier((message, grads.T))
    arrived = lax.all_to_all(message, "z", 0, 0, tiled=True)
    slabs = call(
        dense_down_kernel,
        (slab,) * along,
        place,
        dense_down.T,
        dense_rows,
        scratch=[blocks],
        spaces=[smem, vmem, vmem],
    )
    slabs = [slabs[0]] + [moved(slabs[step], 0, step, along) for step in steps]
    arrived = lax.all_gather(arrived, "c", axis=0, tiled=False)
    arrived, slabs = lax.optimization_barrier((arrived, slabs))

    parts_out = jax.ShapeDtypeStruct((parts, piece, slots), BF16)
    mid = call(
        down_kernel,
        parts_out,
        arrived,
        expert_down[0].T,
        scratch=[pltpu.VMEM((parts, piece, slots), BF16), pltpu.SemaphoreType.DMA((parts,))],
        out_space=pltpu.HBM,
    )
    mid, slabs = lax.optimization_barrier((mid, slabs))
    shares = lax.all_to_all(mid, tensor, 0, 0, tiled=True)
    sums = call(
        dense_sum_kernel,
        (piece_f32,) + (piece_bf16,) * (along - 1),
        place,
        *slabs,
        spaces=[smem] + [vmem] * along,
    )
    pieces = [sums[0]] + [moved(sums[step], 1, step, along) for step in steps]
    shares, pieces = lax.optimization_barrier((shares, pieces))
    copies = call(
        gate_kernel,
        parts_out,
        shares,
        expert_act[0].T,
        scratch=[pltpu.VMEM((piece, slots), BF16), pltpu.SemaphoreType.DMA((parts,))],
        out_space=pltpu.HBM,
    )
    copies, pieces, up = lax.optimization_barrier((copies, pieces, expert_up[0]))
    full = lax.all_to_all(copies, tensor, 0, 0, tiled=True)
    up = call(
        hold_kernel,
        jax.ShapeDtypeStruct((width, half), BF16),
        up,
        scratch=[pltpu.SemaphoreType.DMA],
        spaces=[pltpu.HBM],
        room=2,
    )
    full, pieces, up = lax.optimization_barrier((full, pieces, up))
    rows_t = call(
        up_kernel,
        jax.ShapeDtypeStruct((width, slots), BF16),
        full,
        up,
        scratch=[pltpu.VMEM((half, slots), F32)],
    )
    back = call(
        return_kernel,
        jax.ShapeDtypeStruct((held, 2, 3 * width), BF16),
        core.astype(jnp.int32).reshape(1),
        lax.all_gather(rows_t, "c", axis=0, tiled=False),
        spaces=[smem, vmem],
    )
    back, pieces = lax.optimization_barrier((back, pieces))
    returned = lax.all_to_all(back, "z", 0, 0, tiled=True)
    hidden = call(dense_gate_kernel, piece_bf16, *pieces, dense_act.T)
    columns = [hidden] + [moved(hidden, 1, step, along) for step in steps]
    column = jnp.stack(columns)
    dense_t = call(
        dense_up_kernel,
        jax.ShapeDtypeStruct((width, tokens), F32),
        place,
        column,
        *[moved(column, 0, step, along) for step in steps],
        dense_up,
        scratch=[blocks],
        spaces=[smem] + [vmem] * (along + 1),
    )
    out_t = call(
        combine_kernel, jax.ShapeDtypeStruct((width, tokens), BF16), returned, chooser, dense_t
    )
    return out_t.T


def solution(mesh):
    groups, parts = mesh.devices.shape
    across = 4 if parts == 16 else 2
    split = Mesh(
        mesh.devices.reshape(groups // 2, 2, across, parts // across), ("z", "c", "x", "y")
    )
    blocks, tensor = ("z", "c"), ("x", "y")
    placed = (
        P(blocks, tensor),
        P(blocks, None),
        P(blocks, None),
        P(None, tensor),
        P(tensor, None),
        P(blocks, tensor),
        P(blocks, None, tensor),
        P(blocks, tensor, None),
        P(blocks, None, tensor),
    )
    return jax.shard_map(
        shards, mesh=split, in_specs=placed, out_specs=P(blocks, tensor), check_vma=False
    )
```

```python
import jax
import jax.numpy as jnp
from jax import lax
from jax.experimental import pallas as pl
from jax.experimental.pallas import tpu as pltpu
from jax.sharding import Mesh, PartitionSpec as P

CAP = 6
ROOM = 60
F32 = jnp.float32
BF16 = jnp.bfloat16


def call(kernel, outs, *operands, room=20, scratch=(), spaces=None, out_space=pltpu.VMEM):
    size = sum(v.size * v.dtype.itemsize for v in operands)
    spaces = spaces or [pltpu.VMEM] * len(operands)
    return pl.pallas_call(
        kernel,
        out_shape=outs,
        in_specs=[pl.BlockSpec(memory_space=space) for space in spaces],
        out_specs=jax.tree.map(lambda _: pl.BlockSpec(memory_space=out_space), outs),
        scratch_shapes=list(scratch),
        compiler_params=pltpu.CompilerParams(vmem_limit_bytes=room * 1024 * 1024),
        cost_estimate=pl.CostEstimate(flops=0, bytes_accessed=size, transcendentals=0),
    )(*operands)


def dot(left, right, left_dim, right_dim):
    return lax.dot_general(
        left, right, (((left_dim,), (right_dim,)), ((), ())), preferred_element_type=F32
    )


def iota(shape, dim):
    return lax.broadcasted_iota(jnp.int32, shape, dim)


LANES = 128


def packed(rows):
    count, cut = rows.shape[0] // CAP, rows.shape[1] // LANES * LANES
    split = [rows[count * i : count * (i + 1)] for i in range(CAP)]
    sides = [
        jnp.concatenate(
            [row[:, :cut] for row in split[3 * side : 3 * side + 3]]
            + [row[:, cut:] for row in split[3 * side : 3 * side + 3]],
            axis=1,
        )
        for side in range(2)
    ]
    return jnp.stack(sides, axis=1).astype(BF16)


def unpacked(message):
    wide = message.astype(F32)
    width = wide.shape[2] // 3
    cut = width // LANES * LANES
    tail = width - cut
    rows = []
    for side in range(2):
        for i in range(3):
            low = 3 * cut + tail * i
            main = wide[:, side, cut * i : cut * (i + 1)]
            rows.append(jnp.concatenate([main, wide[:, side, low : low + tail]], axis=1))
    return jnp.concatenate(rows, axis=0).astype(BF16)


def dispatch_kernel(routes, gates, grads_t, message, chooser):
    held = message.shape[0]
    tokens = routes.shape[1]
    ids = routes[...]
    experts = iota((held, tokens), 0)
    first, second = ids[0:1] == experts, ids[1:2] == experts
    named = jnp.where(first | second, 1.0, 0.0).astype(BF16)
    before = jnp.where(
        iota((tokens, tokens), 0) < iota((tokens, tokens), 1), 1.0, 0.0
    ).astype(BF16)
    place = experts + dot(named, before, 1, 0).astype(jnp.int32) * held + 1
    row = iota((held * CAP, tokens), 0) + 1
    hit_first = jnp.sum(jnp.where(first, place, 0), axis=0, keepdims=True) == row
    hit_second = jnp.sum(jnp.where(second, place, 0), axis=0, keepdims=True) == row
    weight = gates[...]
    gate = jnp.sum(
        jnp.where(hit_first, weight[0:1], 0.0) + jnp.where(hit_second, weight[1:2], 0.0),
        axis=1,
        keepdims=True,
    )
    chosen = jnp.where(hit_first | hit_second, 1.0, 0.0).astype(BF16)
    chooser[...] = chosen
    message[...] = packed(dot(chosen, grads_t[...], 1, 1) * gate)


def down_kernel(arrived, down_t, mid, held_out, sems):
    cores, held = arrived.shape[0], arrived.shape[1]
    rows = unpacked(arrived[...].reshape((cores * held,) + arrived.shape[2:]))
    slots, sources = rows.shape[0], cores * held
    row = iota((slots, slots), 1)
    rank = row // sources
    source = row - rank * sources
    core = jnp.where(source >= held, 1, 0)
    slot = ((source - core * held) * 2 + core) * CAP + rank
    pick = jnp.where(slot == iota((slots, slots), 0), 1.0, 0.0).astype(BF16)
    picked = dot(pick, rows, 1, 0).astype(BF16)
    total = dot(down_t[...], picked, 0, 1)
    piece = mid.shape[1]
    copies = []
    for part in range(mid.shape[0]):
        held_out[part] = total[piece * part : piece * (part + 1)].astype(BF16)
        copies.append(pltpu.make_async_copy(held_out.at[part], mid.at[part], sems.at[part]))
        copies[part].start()
    for copy in copies:
        copy.wait()


def gate_kernel(shares, act, copies, held_out, sems):
    total = shares[0].astype(F32)
    for part in range(1, shares.shape[0]):
        total = total + shares[part].astype(F32)
    value = act[...].astype(F32)
    held_out[...] = (total * (value / (1.0 + jnp.exp(-value)))).astype(BF16)
    sent = [
        pltpu.make_async_copy(held_out, copies.at[part], sems.at[part])
        for part in range(copies.shape[0])
    ]
    for copy in sent:
        copy.start()
    for copy in sent:
        copy.wait()


def hold_kernel(weights, held_in, sem):
    copy = pltpu.make_async_copy(weights, held_in, sem)
    copy.start()
    copy.wait()


def up_kernel(full, up, rows_t, stacked):
    piece = full.shape[1]
    for part in range(full.shape[0]):
        stacked[piece * part : piece * (part + 1), :] = full[part].astype(F32)
    rows_t[...] = dot(up[...], stacked[...].astype(BF16), 1, 0).astype(BF16)


def return_kernel(core_id, halves, message):
    held = message.shape[0]
    slots = halves.shape[2]
    core = core_id[0]
    both = (halves[0].astype(F32) + halves[1].astype(F32)).astype(BF16)
    row = iota((held * CAP, slots), 0)
    rank = row // held
    slot = ((row - rank * held) * 2 + core) * CAP + rank
    pick = jnp.where(slot == iota((held * CAP, slots), 1), 1.0, 0.0).astype(BF16)
    message[...] = packed(dot(pick, both, 1, 1))


def combine_kernel(returned, chooser, dense_t, out_t):
    routed = dot(unpacked(returned[...]), chooser[...], 0, 0)
    out_t[...] = (dense_t[...] + routed).astype(BF16)


def wrapped(value, size):
    value = jnp.where(value >= size, value - size, value)
    return jnp.where(value < 0, value + size, value)


def dense_down_kernel(place, down_t, grads_t, *rest):
    slabs, blocks = rest[:-1], rest[-1]
    size = len(slabs)
    blocks[...] = dot(down_t[...], grads_t[...], 0, 0).reshape(blocks.shape)
    for step in range(size):
        first = wrapped(place[0] + step, size) * place[2]
        for second in range(size):
            slabs[step][second] = blocks[first + second * place[3]].astype(BF16)


def dense_sum_kernel(place, *rest):
    size = len(rest) // 2
    slabs, sums = rest[:size], rest[size:]
    for step in range(size):
        second = wrapped(place[1] + step, size)
        total = slabs[0][second].astype(F32)
        for slab in slabs[1:]:
            total = total + slab[second].astype(F32)
        sums[step][...] = total.astype(sums[step].dtype)


def dense_gate_kernel(*rest):
    pieces, act, hidden = rest[:-2], rest[-2], rest[-1]
    total = pieces[0][...].astype(F32)
    for piece in pieces[1:]:
        total = total + piece[...].astype(F32)
    value = act[...].astype(F32)
    hidden[...] = (total * (value / (1.0 + jnp.exp(-value)))).astype(BF16)


def dense_up_kernel(place, *rest):
    slabs, up, out_t, blocks = rest[:-3], rest[-3], rest[-2], rest[-1]
    size = len(slabs)
    for back in range(size):
        first = wrapped(place[0] - back, size) * place[2]
        for step in range(size):
            second = wrapped(place[1] - step, size) * place[3]
            blocks[first + second] = slabs[back][step].astype(F32)
    full = blocks[...].reshape(up.shape[1], blocks.shape[2]).astype(BF16)
    out_t[...] = dot(up[...], full, 1, 0)


def moved(value, stage, step, size):
    pairs = []
    for core in range(2):
        for x in range(size):
            for y in range(size):
                if core == stage:
                    target = ((x + step) % size, y)
                else:
                    target = (x, (y + step) % size)
                pairs.append(
                    ((core * size + x) * size + y, (core * size + target[0]) * size + target[1])
                )
    return lax.ppermute(value, ("c", "x", "y"), pairs)


def shards(
    grads, routes, gates, dense_down, dense_up, dense_act, expert_down, expert_up, expert_act
):
    held = lax.axis_size("z")
    across, along = lax.axis_size("x"), lax.axis_size("y")
    parts = across * along
    tokens, width = grads.shape
    half = expert_down.shape[1]
    piece, share = half // parts, dense_act.shape[1]
    slots = expert_act.shape[1]
    tensor = ("x", "y")

    message, chooser = call(
        dispatch_kernel,
        (
            jax.ShapeDtypeStruct((held, 2, 3 * width), BF16),
            jax.ShapeDtypeStruct((held * CAP, tokens), BF16),
        ),
        routes.T,
        gates.T,
        grads.T,
        room=ROOM,
    )
    core, x, y = lax.axis_index("c"), lax.axis_index("x"), lax.axis_index("y")
    place = jnp.stack(
        [
            jnp.where(core == 0, x, y),
            jnp.where(core == 0, y, x),
            jnp.where(core == 0, along, 1),
            jnp.where(core == 0, 1, along),
        ]
    ).astype(jnp.int32)
    smem, vmem = pltpu.SMEM, pltpu.VMEM
    slab = jax.ShapeDtypeStruct((along, share, tokens), BF16)
    piece_f32 = jax.ShapeDtypeStruct((share, tokens), F32)
    piece_bf16 = jax.ShapeDtypeStruct((share, tokens), BF16)
    blocks = pltpu.VMEM((parts, share, tokens), F32)
    steps = range(1, along)

    message, dense_rows = lax.optimization_barrier((message, grads.T))
    arrived = lax.all_to_all(message, "z", 0, 0, tiled=True)
    slabs = call(
        dense_down_kernel,
        (slab,) * along,
        place,
        dense_down.T,
        dense_rows,
        scratch=[blocks],
        spaces=[smem, vmem, vmem],
    )
    slabs = [slabs[0]] + [moved(slabs[step], 0, step, along) for step in steps]
    arrived = lax.all_gather(arrived, "c", axis=0, tiled=False)
    arrived, slabs = lax.optimization_barrier((arrived, slabs))

    parts_out = jax.ShapeDtypeStruct((parts, piece, slots), BF16)
    mid = call(
        down_kernel,
        parts_out,
        arrived,
        expert_down[0].T,
        scratch=[pltpu.VMEM((parts, piece, slots), BF16), pltpu.SemaphoreType.DMA((parts,))],
        out_space=pltpu.HBM,
    )
    mid, slabs = lax.optimization_barrier((mid, slabs))
    shares = lax.all_to_all(mid, tensor, 0, 0, tiled=True)
    sums = call(
        dense_sum_kernel,
        (piece_f32,) + (piece_bf16,) * (along - 1),
        place,
        *slabs,
        spaces=[smem] + [vmem] * along,
    )
    pieces = [sums[0]] + [moved(sums[step], 1, step, along) for step in steps]
    shares, pieces = lax.optimization_barrier((shares, pieces))
    copies = call(
        gate_kernel,
        parts_out,
        shares,
        expert_act[0].T,
        scratch=[pltpu.VMEM((piece, slots), BF16), pltpu.SemaphoreType.DMA((parts,))],
        out_space=pltpu.HBM,
    )
    copies, pieces, up = lax.optimization_barrier((copies, pieces, expert_up[0]))
    full = lax.all_to_all(copies, tensor, 0, 0, tiled=True)
    up = call(
        hold_kernel,
        jax.ShapeDtypeStruct((width, half), BF16),
        up,
        scratch=[pltpu.SemaphoreType.DMA],
        spaces=[pltpu.HBM],
        room=2,
    )
    full, pieces, up = lax.optimization_barrier((full, pieces, up))
    rows_t = call(
        up_kernel,
        jax.ShapeDtypeStruct((width, slots), BF16),
        full,
        up,
        scratch=[pltpu.VMEM((half, slots), F32)],
    )
    back = call(
        return_kernel,
        jax.ShapeDtypeStruct((held, 2, 3 * width), BF16),
        core.astype(jnp.int32).reshape(1),
        lax.all_gather(rows_t, "c", axis=0, tiled=False),
        spaces=[smem, vmem],
    )
    back, pieces = lax.optimization_barrier((back, pieces))
    returned = lax.all_to_all(back, "z", 0, 0, tiled=True)
    hidden = call(dense_gate_kernel, piece_bf16, *pieces, dense_act.T)
    columns = [hidden] + [moved(hidden, 1, step, along) for step in steps]
    column = jnp.stack(columns)
    dense_t = call(
        dense_up_kernel,
        jax.ShapeDtypeStruct((width, tokens), F32),
        place,
        column,
        *[moved(column, 0, step, along) for step in steps],
        dense_up,
        scratch=[blocks],
        spaces=[smem] + [vmem] * (along + 1),
    )
    out_t = call(
        combine_kernel, jax.ShapeDtypeStruct((width, tokens), BF16), returned, chooser, dense_t
    )
    return out_t.T


def solution(mesh):
    groups, parts = mesh.devices.shape
    across = 4 if parts == 16 else 2
    split = Mesh(
        mesh.devices.reshape(groups // 2, 2, across, parts // across), ("z", "c", "x", "y")
    )
    blocks, tensor = ("z", "c"), ("x", "y")
    placed = (
        P(blocks, tensor),
        P(blocks, None),
        P(blocks, None),
        P(None, tensor),
        P(tensor, None),
        P(blocks, tensor),
        P(blocks, None, tensor),
        P(blocks, tensor, None),
        P(blocks, None, tensor),
    )
    return jax.shard_map(
        shards, mesh=split, in_specs=placed, out_specs=P(blocks, tensor), check_vma=False
    )
```
